32 devices in a mesh: wide: 16 (over z, y, x), narrow: 2 (over core).
Axes of the slice: x: 2, y: 2, z: 4, core: 2. Of those that a mesh axis runs over, the one named last changes fastest.
Arguments:
- primal_in: bfloat16 [32, 8192], P('wide', 'narrow'), may hold values from -6 to 6
- tangent_in: bfloat16 [32, 8192], P('wide', 'narrow'), may hold values from -6 to 6
- cotangent: bfloat16 [32, 8192], P('wide', 'narrow'), may hold values from -6 to 6
- gate_weight: bfloat16 [8192, 2048], P('narrow', 'wide'), may hold values from -0.0625 to 0.0625
- up_weight: bfloat16 [8192, 2048], P('narrow', 'wide'), may hold values from -0.0625 to 0.0625
- down_weight: bfloat16 [2048, 8192], P('wide', 'narrow'), may hold values from -0.125 to 0.125
Outputs:
- input_hvp: bfloat16 [32, 8192], P('wide', 'narrow')
- gate_grad_tangent: float32 [8192, 2048], P('narrow', 'wide')
- up_grad_tangent: float32 [8192, 2048], P('narrow', 'wide')
- down_grad_tangent: float32 [2048, 8192], P('wide', 'narrow')
The draws below stay inside these ranges and needn't reach their ends.
All inputs are finite; a program needn't handle non-finite values.
Results may differ from the reference program's by a relative error of at most 0.0049.
Values may be sent and summed in bfloat16 or wider, within the bound.
No kernel may reach another device: no remote copies, remote signals or barrier semaphores. Data moves between devices by JAX's collectives and lax.ppermute only.
A program may use at most 64 MiB of HBM per device.

```python
import jax
import jax.numpy as jnp
from jax import lax

D = 8192
HIDDEN_SIZE = 2048
TOKENS = 32


def steps_of(rng, shape, split, smallest, largest):
    gain = 1.0
    for dim, shards_of in split:
        heights = jax.random.uniform(jax.random.fold_in(jax.random.fold_in(rng, 6), dim), (shards_of,), jnp.float32, smallest / len(split), largest / len(split))
        gain = gain * jnp.repeat(jnp.exp(heights), shape[dim] // shards_of).reshape((-1,) + (1,) * (len(shape) - 1 - dim))
    return gain


def bell_draw(key, shape, width, limit, cuts=(), kind=jnp.bfloat16):
    result = width * jax.random.normal(key, shape, jnp.float32)
    if cuts:
        result = result * steps_of(key, shape, cuts, -0.22, 0.18)
    return jnp.clip(result, -limit, limit).astype(kind)


def setup_inputs(seed: int = 0) -> dict:
    key_of = jax.random.split(jax.random.key(seed), 7)
    primal_in = bell_draw(key_of[0], (TOKENS, D), 1.0, 6.0, ((0, 16), (1, 2)))
    tangent_in = bell_draw(key_of[1], (TOKENS, D), 1.0, 6.0, ((0, 16), (1, 2)))
    cotangent = bell_draw(key_of[2], (TOKENS, D), 1.0, 6.0, ((0, 16), (1, 2)))
    gate_weight = bell_draw(key_of[3], (D, HIDDEN_SIZE), D ** -0.5, 0.0625, ((0, 2), (1, 16)))
    up_weight = bell_draw(key_of[4], (D, HIDDEN_SIZE), D ** -0.5, 0.0625, ((0, 2), (1, 16)))
    down_weight = bell_draw(key_of[5], (HIDDEN_SIZE, D), HIDDEN_SIZE ** -0.5, 0.125, ((0, 16), (1, 2)))
    return {"primal_in": primal_in, "tangent_in": tangent_in, "cotangent": cotangent, "gate_weight": gate_weight, "up_weight": up_weight, "down_weight": down_weight}


def contract_first(left, right):
    return lax.dot_general(left, right, (((0,), (0,)), ((), ())), preferred_element_type=jnp.float32)


def contract_last(left, right):
    return lax.dot_general(left, right, (((1,), (1,)), ((), ())), preferred_element_type=jnp.float32)


def factors(gate, up, tgate, tup, dact):
    sig = jax.nn.sigmoid(gate)
    act = gate * sig
    first = sig * (1.0 + gate * (1.0 - sig))
    second = sig * (1.0 - sig) * (2.0 + gate * (1.0 - 2.0 * sig))
    dgate = (dact * up * first).astype(jnp.bfloat16)
    dup = (dact * act).astype(jnp.bfloat16)
    tdgate = (dact * (tup * first + up * second * tgate)).astype(jnp.bfloat16)
    tdup = (dact * first * tgate).astype(jnp.bfloat16)
    tact = (tgate * first * up + act * tup).astype(jnp.bfloat16)
    return dgate, dup, tdgate, tdup, tact


def reference(primal_in, tangent_in, cotangent, gate_weight, up_weight, down_weight):
    gate = jnp.dot(primal_in, gate_weight, preferred_element_type=jnp.float32)
    up = jnp.dot(primal_in, up_weight, preferred_element_type=jnp.float32)
    tgate = jnp.dot(tangent_in, gate_weight, preferred_element_type=jnp.float32)
    tup = jnp.dot(tangent_in, up_weight, preferred_element_type=jnp.float32)
    dact = contract_last(cotangent, down_weight)
    dgate, dup, tdgate, tdup, tact = factors(gate, up, tgate, tup, dact)
    input_hvp = (contract_last(tdgate, gate_weight) + contract_last(tdup, up_weight)).astype(jnp.bfloat16)
    gate_grad = contract_first(tangent_in, dgate) + contract_first(primal_in, tdgate)
    up_grad = contract_first(tangent_in, dup) + contract_first(primal_in, tdup)
    down_grad = contract_first(tact, cotangent)
    return (input_hvp, gate_grad, up_grad, down_grad)
```

```python
import jax
import jax.numpy as jnp
from jax import lax
from jax.sharding import PartitionSpec as P


def levels_of(size):
    levels, stride = [], 1
    while stride < size:
        rest = size // stride
        radix = next(r for r in (4, 2, 3, 5, 7, rest) if rest % r == 0)
        levels.append((stride, radix))
        stride *= radix
    return levels[::-1]


def partner(index, stride, radix, offset):
    digit = index // stride % radix
    if radix & (radix - 1) == 0:
        other = digit ^ offset
    else:
        other = (digit + offset) % radix
    return index + (other - digit) * stride


def fetch(value, axis, size, stride, radix, offset):
    pairs = [(partner(i, stride, radix, offset), i) for i in range(size)]
    return lax.ppermute(value, axis, pairs)


def deliver(value, axis, size, stride, radix, offset):
    pairs = [(i, partner(i, stride, radix, offset)) for i in range(size)]
    return lax.ppermute(value, axis, pairs)


def gather_rows(rows, axis, size):
    for stride, radix in levels_of(size):
        rows = jnp.concatenate(
            [rows]
            + [fetch(rows, axis, size, stride, radix, o) for o in range(1, radix)]
        )
    return rows


def scatter_sum(rows, axis, size):
    for stride, radix in levels_of(size)[::-1]:
        parts = jnp.split(rows, radix)
        rows = parts[0]
        for o in range(1, radix):
            rows = rows + deliver(parts[o], axis, size, stride, radix, o)
    return rows


def contract_first(left, right):
    return lax.dot_general(
        left, right, (((0,), (0,)), ((), ())), preferred_element_type=jnp.float32
    )


def contract_last(left, right):
    return lax.dot_general(
        left, right, (((1,), (1,)), ((), ())), preferred_element_type=jnp.float32
    )


def factors(gate, up, tgate, tup, dact):
    sig = jax.nn.sigmoid(gate)
    act = gate * sig
    first = sig * (1.0 + gate * (1.0 - sig))
    second = sig * (1.0 - sig) * (2.0 + gate * (1.0 - 2.0 * sig))
    dgate = (dact * up * first).astype(jnp.bfloat16)
    dup = (dact * act).astype(jnp.bfloat16)
    tdgate = (dact * (tup * first + up * second * tgate)).astype(jnp.bfloat16)
    tdup = (dact * first * tgate).astype(jnp.bfloat16)
    tact = (tgate * first * up + act * tup).astype(jnp.bfloat16)
    return (dgate, dup, tdgate, tdup, tact)


def solution(mesh):
    wide, narrow = mesh.shape["wide"], mesh.shape["narrow"]

    def local(primal_in, tangent_in, cotangent, gate_weight, up_weight, down_weight):
        width = primal_in.shape[1]
        rows = gather_rows(
            jnp.concatenate([primal_in, tangent_in, cotangent], axis=1), "wide", wide
        )
        primal, tangent, cotan = (
            rows[:, k * width : (k + 1) * width] for k in range(3)
        )
        parts = jnp.stack(
            [
                jnp.dot(primal, gate_weight, preferred_element_type=jnp.float32),
                jnp.dot(primal, up_weight, preferred_element_type=jnp.float32),
                jnp.dot(tangent, gate_weight, preferred_element_type=jnp.float32),
                jnp.dot(tangent, up_weight, preferred_element_type=jnp.float32),
                contract_last(cotan, down_weight),
            ]
        )
        total = parts
        for shift in range(1, narrow):
            pairs = [(i, (i + shift) % narrow) for i in range(narrow)]
            total = total + lax.ppermute(parts, "narrow", pairs)
        dgate, dup, tdgate, tdup, tact = factors(*total)
        input_hvp = scatter_sum(
            contract_last(tdgate, gate_weight) + contract_last(tdup, up_weight),
            "wide",
            wide,
        ).astype(jnp.bfloat16)
        gate_grad = contract_first(tangent, dgate) + contract_first(primal, tdgate)
        up_grad = contract_first(tangent, dup) + contract_first(primal, tdup)
        down_grad = contract_first(tact, cotan)
        return (input_hvp, gate_grad, up_grad, down_grad)

    return jax.shard_map(
        local,
        mesh=mesh,
        in_specs=(
            P("wide", "narrow"),
            P("wide", "narrow"),
            P("wide", "narrow"),
            P("narrow", "wide"),
            P("narrow", "wide"),
            P("wide", "narrow"),
        ),
        out_specs=(
            P("wide", "narrow"),
            P("narrow", "wide"),
            P("narrow", "wide"),
            P("wide", "narrow"),
        ),
        check_vma=False,
    )
```

```python
import jax
import jax.numpy as jnp
from jax import lax
from jax.sharding import PartitionSpec as P


def levels_of(size):
    levels, stride = [], 1
    while stride < size:
        rest = size // stride
        radix = next(r for r in (4, 2, 3, 5, 7, rest) if rest % r == 0)
        levels.append((stride, radix))
        stride *= radix
    return levels[::-1]


def partner(index, stride, radix, offset):
    digit = index // stride % radix
    if radix & (radix - 1) == 0:
        other = digit ^ offset
    else:
        other = (digit + offset) % radix
    return index + (other - digit) * stride


def fetch(value, axis, size, stride, radix, offset):
    pairs = [(partner(i, stride, radix, offset), i) for i in range(size)]
    return lax.ppermute(value, axis, pairs)


def deliver(value, axis, size, stride, radix, offset):
    pairs = [(i, partner(i, stride, radix, offset)) for i in range(size)]
    return lax.ppermute(value, axis, pairs)


def gather_blocks(own, axis, size):
    rest = []
    for stride, radix in levels_of(size):
        held = jnp.concatenate(rest) if rest else None
        came = []
        for o in range(1, radix):
            came.append(fetch(own, axis, size, stride, radix, o))
            if rest:
                came.append(fetch(held, axis, size, stride, radix, o))
        rest = ([held] if rest else []) + came
    return jnp.concatenate([own] + rest)


def scatter_sum(rows, axis, size):
    for stride, radix in levels_of(size)[::-1]:
        parts = jnp.split(rows, radix)
        rows = parts[0]
        for o in range(1, radix):
            came = deliver(
                parts[o].astype(jnp.bfloat16), axis, size, stride, radix, o
            )
            rows = rows + came.astype(jnp.float32)
    return rows


def contract_first(left, right):
    return lax.dot_general(
        left, right, (((0,), (0,)), ((), ())), preferred_element_type=jnp.float32
    )


def contract_last(left, right):
    return lax.dot_general(
        left, right, (((1,), (1,)), ((), ())), preferred_element_type=jnp.float32
    )


def factors(gate, up, tgate, tup, dact):
    sig = jax.nn.sigmoid(gate)
    act = gate * sig
    first = sig * (1.0 + gate * (1.0 - sig))
    second = sig * (1.0 - sig) * (2.0 + gate * (1.0 - 2.0 * sig))
    dgate = (dact * up * first).astype(jnp.bfloat16)
    dup = (dact * act).astype(jnp.bfloat16)
    tdgate = (dact * (tup * first + up * second * tgate)).astype(jnp.bfloat16)
    tdup = (dact * first * tgate).astype(jnp.bfloat16)
    tact = (tgate * first * up + act * tup).astype(jnp.bfloat16)
    return (dgate, dup, tdgate, tdup, tact)


def solution(mesh):
    wide, narrow = mesh.shape["wide"], mesh.shape["narrow"]

    def local(primal_in, tangent_in, cotangent, gate_weight, up_weight, down_weight):
        block = jnp.stack([primal_in, tangent_in, cotangent])[None]
        blocks = gather_blocks(block, "wide", wide)
        primal, tangent, cotan = (
            blocks[:, k].reshape(-1, primal_in.shape[1]) for k in range(3)
        )
        parts = jnp.stack(
            [
                jnp.dot(primal, gate_weight, preferred_element_type=jnp.float32),
                jnp.dot(primal, up_weight, preferred_element_type=jnp.float32),
                jnp.dot(tangent, gate_weight, preferred_element_type=jnp.float32),
                jnp.dot(tangent, up_weight, preferred_element_type=jnp.float32),
                contract_last(cotan, down_weight),
            ]
        )
        total = parts
        for shift in range(1, narrow):
            pairs = [(i, (i + shift) % narrow) for i in range(narrow)]
            total = total + lax.ppermute(parts, "narrow", pairs)
        dgate, dup, tdgate, tdup, tact = factors(*total)
        input_hvp = scatter_sum(
            contract_last(tdgate, gate_weight) + contract_last(tdup, up_weight),
            "wide",
            wide,
        ).astype(jnp.bfloat16)
        gate_grad = contract_first(tangent, dgate) + contract_first(primal, tdgate)
        up_grad = contract_first(tangent, dup) + contract_first(primal, tdup)
        down_grad = contract_first(tact, cotan)
        return (input_hvp, gate_grad, up_grad, down_grad)

    return jax.shard_map(
        local,
        mesh=mesh,
        in_specs=(
            P("wide", "narrow"),
            P("wide", "narrow"),
            P("wide", "narrow"),
            P("narrow", "wide"),
            P("narrow", "wide"),
            P("wide", "narrow"),
        ),
        out_specs=(
            P("wide", "narrow"),
            P("narrow", "wide"),
            P("narrow", "wide"),
            P("wide", "narrow"),
        ),
        check_vma=False,
    )
```

```python
import functools

import jax
import jax.numpy as jnp
from jax import lax
from jax.experimental import pallas as pl
from jax.experimental.pallas import tpu as pltpu
from jax.sharding import PartitionSpec as P

SLOTS = 4
LANES = 128


def levels_of(size):
    levels, stride = [], 1
    while stride < size:
        rest = size // stride
        radix = next(r for r in (4, 2, 3, 5, 7, rest) if rest % r == 0)
        levels.append((stride, radix))
        stride *= radix
    return levels[::-1]


def partner(index, stride, radix, offset):
    digit = index // stride % radix
    if radix & (radix - 1) == 0:
        other = digit ^ offset
    else:
        other = (digit + offset) % radix
    return index + (other - digit) * stride


def fetch(value, axis, size, level, offset):
    pairs = [(partner(i, *level, offset), i) for i in range(size)]
    return lax.ppermute(value, axis, pairs)


def deliver(value, axis, size, level, offset):
    pairs = [(i, partner(i, *level, offset)) for i in range(size)]
    return lax.ppermute(value, axis, pairs)


def gather_blocks(own, axis, size):
    rest = []
    for level in levels_of(size):
        offsets = range(level[1] - 1, 0, -1)
        held = jnp.concatenate(rest) if rest else None
        mine = {o: [fetch(own, axis, size, level, o)] for o in offsets}
        if rest:
            for o in offsets:
                mine[o].append(fetch(held, axis, size, level, o))
        rest = ([held] if rest else []) + sum((mine[o] for o in offsets[::-1]), [])
    return [own] + rest


def scatter_sum(groups, axis, size):
    for level in levels_of(size)[::-1]:
        if len(groups) == 1:
            groups = jnp.split(groups[0], level[1])
        total = groups[0]
        for o in range(1, level[1]):
            sent = groups[o].astype(jnp.bfloat16)
            total = total + deliver(sent, axis, size, level, o).astype(jnp.float32)
        groups = [total]
    return groups[0]


def fold_kernel(*refs):
    *rows, out = refs
    for k, ref in enumerate(rows):
        tokens, width = ref.shape
        split = ref[...].reshape(tokens, width // (SLOTS * LANES), SLOTS, LANES)
        for s in range(SLOTS):
            at = (k * SLOTS + s) * tokens
            out[0, at : at + tokens] = split[:, :, s].reshape(tokens, width // SLOTS)


def fold(*rows):
    tokens, width = rows[0].shape
    shape = (1, len(rows) * SLOTS * tokens, width // SLOTS)
    vmem = pl.BlockSpec(memory_space=pltpu.VMEM)
    return pl.pallas_call(
        fold_kernel,
        out_shape=jax.ShapeDtypeStruct(shape, rows[0].dtype),
        in_specs=[vmem] * len(rows),
        out_specs=vmem,
    )(*rows)


def unfold(rows):
    tokens = rows.shape[0] // SLOTS
    split = rows.reshape(SLOTS, tokens, rows.shape[1] // LANES, LANES)
    return split.transpose(1, 2, 0, 3).reshape(tokens, rows.shape[1] * SLOTS)


def slot_of(shape, axis):
    return lax.broadcasted_iota(jnp.int32, shape, axis) // 2


def rows_for_slot(weight, slot):
    height, width = weight.shape
    split = weight.reshape(height // (SLOTS * LANES), SLOTS, LANES, width)
    return split[:, slot].reshape(height // SLOTS, width)


def over_slots(x):
    axis = x.ndim - 2
    x = x + pltpu.roll(x, 4, axis)
    return x + pltpu.roll(x, 2, axis)


def pick_slots(parts):
    slot = slot_of(parts[0].shape, parts[0].ndim - 2)
    result = parts[0]
    for s in range(1, SLOTS):
        result = jnp.where(slot == s, parts[s], result)
    return result


def only_slot(x, s):
    return jnp.where(slot_of(x.shape, x.ndim - 2) == s, x, 0.0)


def forward_kernel(n_pieces, *refs):
    pieces, (gate_w, up_w, down_w), (pt_out, c_out, parts_out) = (
        refs[:n_pieces],
        refs[n_pieces : n_pieces + 3],
        refs[n_pieces + 3 :],
    )
    start = 0
    for piece in pieces:
        count = piece.shape[0]
        for i in range(count):
            at = start + i
            pt_out[at * 16 : at * 16 + 16] = piece[i, 0:16]
            c_out[at * 8 : at * 8 + 8] = piece[i, 16:24]
        start += count
    blocks = start
    pt = pt_out[...]
    cot = c_out[...]
    hidden = gate_w.shape[1]
    acts, dacts = [], []
    for s in range(SLOTS):
        weights = jnp.concatenate(
            [rows_for_slot(gate_w[...], s), rows_for_slot(up_w[...], s)], axis=1
        )
        acts.append(
            jnp.dot(pt, weights, preferred_element_type=jnp.float32).reshape(
                2 * blocks, 8, 2 * hidden
            )
        )
        columns = [
            down_w[:, j * LANES : (j + 1) * LANES]
            for j in range(s, down_w.shape[1] // LANES, SLOTS)
        ]
        dacts.append(
            lax.dot_general(
                cot,
                jnp.concatenate(columns, axis=1),
                (((1,), (1,)), ((), ())),
                preferred_element_type=jnp.float32,
            ).reshape(blocks, 8, hidden)
        )
    act = over_slots(pick_slots(acts)).reshape(blocks, 2, 8, 2 * hidden)
    parts_out[0] = pick_slots(
        [
            act[:, 0, :, :hidden],
            act[:, 0, :, hidden:],
            act[:, 1, :, :hidden],
            act[:, 1, :, hidden:],
        ]
    )
    parts_out[1] = over_slots(pick_slots(dacts))


def forward(pieces, gate_w, up_w, down_w):
    blocks = sum(p.shape[0] for p in pieces)
    lanes, hidden = pieces[0].shape[2], gate_w.shape[1]
    vmem = pl.BlockSpec(memory_space=pltpu.VMEM)
    return pl.pallas_call(
        functools.partial(forward_kernel, len(pieces)),
        out_shape=(
            jax.ShapeDtypeStruct((blocks * 16, lanes), jnp.bfloat16),
            jax.ShapeDtypeStruct((blocks * 8, lanes), jnp.bfloat16),
            jax.ShapeDtypeStruct((2, blocks, 8, hidden), jnp.float32),
        ),
        in_specs=[vmem] * (len(pieces) + 3),
        out_specs=(vmem,) * 3,
        compiler_params=pltpu.CompilerParams(vmem_limit_bytes=40 * 2**20),
    )(*pieces, gate_w, up_w, down_w)


def factors(gate, up, tgate, tup, dact):
    sig = 1.0 / (1.0 + jnp.exp(-gate))
    act = gate * sig
    first = sig * (1.0 + gate * (1.0 - sig))
    second = sig * (1.0 - sig) * (2.0 + gate * (1.0 - 2.0 * sig))
    dgate = dact * up * first
    dup = dact * act
    tdgate = dact * (tup * first + up * second * tgate)
    tdup = dact * first * tgate
    tact = tgate * first * up + act * tup
    return (dgate, dup, tdgate, tdup, tact)


def middle_kernel(n_parts, groups, *refs):
    parts, (gate_w, up_w) = refs[:n_parts], refs[n_parts : n_parts + 2]
    factor_out, tact_out = refs[n_parts + 2 : n_parts + 4]
    own_out, others_out = refs[n_parts + 4], refs[n_parts + 5 :]
    packed, dact = (sum(p[k] for p in parts[1:]) + parts[0][k] for k in range(2))
    gate, up, tgate, tup = (over_slots(only_slot(packed, s)) for s in range(SLOTS))
    dgate, dup, tdgate, tdup, tact = factors(gate, up, tgate, tup, dact)
    blocks, _, hidden = gate.shape
    second = jnp.concatenate([tdgate, tdup], axis=2)
    factor_out[...] = (
        jnp.stack([second, jnp.concatenate([dgate, dup], axis=2)], axis=1)
        .reshape(blocks * 16, 2 * hidden)
        .astype(jnp.bfloat16)
    )
    tact_out[...] = tact.reshape(blocks * 8, hidden).astype(jnp.bfloat16)
    left = jnp.concatenate(
        [
            only_slot(second, s).reshape(blocks * 8, 2 * hidden).astype(jnp.bfloat16)
            for s in range(SLOTS)
        ],
        axis=1,
    )
    right = jnp.concatenate(
        [rows_for_slot(w[...], s) for s in range(SLOTS) for w in (gate_w, up_w)], axis=1
    )
    hvp = lax.dot_general(
        left, right, (((1,), (1,)), ((), ())), preferred_element_type=jnp.float32
    )
    hvp = hvp.reshape(groups, blocks // groups, 8, hvp.shape[1])
    own_out[...] = hvp[0]
    for g, out in enumerate(others_out):
        out[...] = hvp[g + 1].astype(out.dtype)


def middle(parts, gate_w, up_w, groups):
    _, blocks, _, hidden = parts[0].shape
    lanes = gate_w.shape[0] // SLOTS
    vmem = pl.BlockSpec(memory_space=pltpu.VMEM)
    group = (blocks // groups, 8, lanes)
    return pl.pallas_call(
        functools.partial(middle_kernel, len(parts), groups),
        out_shape=(
            jax.ShapeDtypeStruct((blocks * 16, 2 * hidden), jnp.bfloat16),
            jax.ShapeDtypeStruct((blocks * 8, hidden), jnp.bfloat16),
            jax.ShapeDtypeStruct(group, jnp.float32),
        )
        + (jax.ShapeDtypeStruct(group, jnp.bfloat16),) * (groups - 1),
        in_specs=[vmem] * (len(parts) + 2),
        out_specs=(vmem,) * (groups + 2),
        compiler_params=pltpu.CompilerParams(vmem_limit_bytes=40 * 2**20),
    )(*parts, gate_w, up_w)


def only_slot_rows(x, s):
    rows = lax.broadcasted_iota(jnp.int32, x.shape, 0)
    return jnp.where(rows % 8 // 2 == s, x.astype(jnp.float32), 0.0).astype(x.dtype)


def contract_first(left, right):
    return lax.dot_general(
        left, right, (((0,), (0,)), ((), ())), preferred_element_type=jnp.float32
    )


def grads_kernel(pt, cot, factor, tact, gate_out, up_out, down_out):
    hidden = tact.shape[1]
    for s in range(SLOTS):
        both = contract_first(pt[...], only_slot_rows(factor[...], s))
        gate_out[s * LANES : (s + 1) * LANES] = both[:, :hidden]
        up_out[s * LANES : (s + 1) * LANES] = both[:, hidden:]
        down_out[:, s * LANES : (s + 1) * LANES] = contract_first(
            only_slot_rows(tact[...], s), cot[...]
        )


def grads(pt, cot, factor, tact):
    hidden = tact.shape[1]
    tiles = pt.shape[1] // LANES
    width = tiles * SLOTS * LANES
    wide = SLOTS * LANES
    up = jax.ShapeDtypeStruct((width, hidden), jnp.float32)
    return pl.pallas_call(
        grads_kernel,
        grid=(tiles,),
        out_shape=(up, up, jax.ShapeDtypeStruct((hidden, width), jnp.float32)),
        in_specs=[
            pl.BlockSpec((pt.shape[0], LANES), lambda m: (0, m)),
            pl.BlockSpec((cot.shape[0], LANES), lambda m: (0, m)),
            pl.BlockSpec(factor.shape, lambda m: (0, 0)),
            pl.BlockSpec(tact.shape, lambda m: (0, 0)),
        ],
        out_specs=(
            pl.BlockSpec((wide, hidden), lambda m: (m, 0)),
            pl.BlockSpec((wide, hidden), lambda m: (m, 0)),
            pl.BlockSpec((hidden, wide), lambda m: (0, m)),
        ),
        compiler_params=pltpu.CompilerParams(vmem_limit_bytes=40 * 2**20),
    )(pt, cot, factor, tact)


def solution(mesh):
    wide, narrow = mesh.shape["wide"], mesh.shape["narrow"]

    def local(primal_in, tangent_in, cotangent, gate_weight, up_weight, down_weight):
        pieces = gather_blocks(fold(primal_in, tangent_in, cotangent), "wide", wide)
        pt, cot, part = forward(pieces, gate_weight, up_weight, down_weight)
        parts = [part]
        for shift in range(1, narrow):
            pairs = [(i, (i + shift) % narrow) for i in range(narrow)]
            parts.append(lax.ppermute(part, "narrow", pairs))
        groups = levels_of(wide)[-1][1]
        factor, tact, *hvp = middle(parts, gate_weight, up_weight, groups)
        total = scatter_sum(hvp, "wide", wide)
        input_hvp = unfold(total[0].astype(jnp.bfloat16))
        return (input_hvp, *grads(pt, cot, factor, tact))

    return jax.shard_map(
        local,
        mesh=mesh,
        in_specs=(
            P("wide", "narrow"),
            P("wide", "narrow"),
            P("wide", "narrow"),
            P("narrow", "wide"),
            P("narrow", "wide"),
            P("wide", "narrow"),
        ),
        out_specs=(
            P("wide", "narrow"),
            P("narrow", "wide"),
            P("narrow", "wide"),
            P("wide", "narrow"),
        ),
        check_vma=False,
    )
```

```python
import functools

import jax
import jax.numpy as jnp
from jax import lax
from jax.experimental import pallas as pl
from jax.experimental.pallas import tpu as pltpu
from jax.sharding import PartitionSpec as P

SLOTS = 4
LANES = 128
VMEM_LIMIT = 24 * 2**20


def levels_of(size):
    levels, stride = [], 1
    while stride < size:
        rest = size // stride
        radix = next(r for r in (4, 2, 3, 5, 7, rest) if rest % r == 0)
        levels.append((stride, radix))
        stride *= radix
    return levels[::-1]


def partner(index, stride, radix, offset):
    digit = index // stride % radix
    if radix & (radix - 1) == 0:
        other = digit ^ offset
    else:
        other = (digit + offset) % radix
    return index + (other - digit) * stride


def fetch(value, axis, size, level, offset):
    pairs = [(partner(i, *level, offset), i) for i in range(size)]
    return lax.ppermute(value, axis, pairs)


def deliver(value, axis, size, level, offset):
    pairs = [(i, partner(i, *level, offset)) for i in range(size)]
    return lax.ppermute(value, axis, pairs)


def after(value, earlier):
    return lax.optimization_barrier((value, earlier))[0]


def gather_blocks(own, axis, size):
    early, late = [own], []
    for level in levels_of(size):
        early, late = early + late, []
        rest = early[1:]
        offsets = range(level[1] - 1, 0, -1)
        held = jnp.concatenate(rest) if rest else None
        mine = [fetch(own, axis, size, level, o) for o in offsets][::-1]
        if rest:
            late = [
                fetch(after(held, mine[o - 1]), axis, size, level, o) for o in offsets
            ][::-1]
            early = [own, held]
            if level[0] > 1:
                late = [x for pair in zip(mine, late) for x in pair]
                mine = []
        early = early + mine
    return early, late


def scatter_sum(groups, axis, size):
    for level in levels_of(size)[::-1]:
        if len(groups) == 1:
            groups = jnp.split(groups[0], level[1])
        total = groups[0]
        for o in range(1, level[1]):
            sent = groups[o].astype(jnp.bfloat16)
            total = total + deliver(sent, axis, size, level, o).astype(jnp.float32)
        groups = [total]
    return groups[0]


def fold(*rows):
    stacked = lax.optimization_barrier(jnp.stack(rows))
    count, tokens, width = stacked.shape
    split = stacked.reshape(count, tokens, width // (SLOTS * LANES), SLOTS, LANES)
    return split.transpose(0, 3, 1, 2, 4).reshape(1, -1, width // SLOTS)


def unfold(rows):
    tokens = rows.shape[0] // SLOTS
    split = rows.reshape(SLOTS, tokens, rows.shape[1] // LANES, LANES)
    return split.transpose(1, 2, 0, 3).reshape(tokens, rows.shape[1] * SLOTS)


def slot_of(shape, axis):
    return lax.broadcasted_iota(jnp.int32, shape, axis) // 2


def rows_for_slot(weight, slot):
    height, width = weight.shape
    split = weight.reshape(height // (SLOTS * LANES), SLOTS, LANES, width)
    return split[:, slot].reshape(height // SLOTS, width)


def over_slots(x):
    axis = x.ndim - 2
    x = x + pltpu.roll(x, 4, axis)
    return x + pltpu.roll(x, 2, axis)


def pick_slots(parts):
    slot = slot_of(parts[0].shape, parts[0].ndim - 2)
    result = parts[0]
    for s in range(1, SLOTS):
        result = jnp.where(slot == s, parts[s], result)
    return result


def only_slot(x, s):
    return jnp.where(slot_of(x.shape, x.ndim - 2) == s, x, 0.0)


def place(pieces, at, pt_out, c_out):
    for piece in pieces:
        for i in range(piece.shape[0]):
            pt_out[at * 16 : at * 16 + 16] = piece[i, 0:16]
            c_out[at * 8 : at * 8 + 8] = piece[i, 16:24]
            at += 1


def projections(pt, cot, gate_w, up_w, down_w):
    blocks, hidden = cot.shape[0] // 8, gate_w.shape[1]
    acts, dacts = [], []
    for s in range(SLOTS):
        weights = jnp.concatenate(
            [rows_for_slot(gate_w[...], s), rows_for_slot(up_w[...], s)], axis=1
        )
        acts.append(
            jnp.dot(pt, weights, preferred_element_type=jnp.float32).reshape(
                2 * blocks, 8, 2 * hidden
            )
        )
        columns = [
            down_w[:, j * LANES : (j + 1) * LANES]
            for j in range(s, down_w.shape[1] // LANES, SLOTS)
        ]
        dacts.append(
            lax.dot_general(
                cot,
                jnp.concatenate(columns, axis=1),
                (((1,), (1,)), ((), ())),
                preferred_element_type=jnp.float32,
            ).reshape(blocks, 8, hidden)
        )
    act = over_slots(pick_slots(acts)).reshape(blocks, 2, 8, 2 * hidden)
    packed = pick_slots(
        [
            act[:, 0, :, :hidden],
            act[:, 0, :, hidden:],
            act[:, 1, :, :hidden],
            act[:, 1, :, hidden:],
        ]
    )
    return packed, over_slots(pick_slots(dacts))


def begin_kernel(n_pieces, *refs):
    pieces, weights = refs[:n_pieces], refs[n_pieces : n_pieces + 3]
    pt_out, c_out, parts_out, *held, sems = refs[n_pieces + 3 :]
    copies = [
        pltpu.make_async_copy(w, h, sems.at[k])
        for k, (w, h) in enumerate(zip(weights, held))
    ]
    for copy in copies:
        copy.start()
    place(pieces, 0, pt_out, c_out)
    for copy in copies:
        copy.wait()
    parts_out[0], parts_out[1] = projections(pt_out[...], c_out[...], *held)


def begin(pieces, weights):
    blocks = sum(p.shape[0] for p in pieces)
    lanes, hidden = pieces[0].shape[2], weights[0].shape[1]
    vmem = pl.BlockSpec(memory_space=pltpu.VMEM)
    return pl.pallas_call(
        functools.partial(begin_kernel, len(pieces)),
        out_shape=(
            jax.ShapeDtypeStruct((blocks * 16, lanes), jnp.bfloat16),
            jax.ShapeDtypeStruct((blocks * 8, lanes), jnp.bfloat16),
            jax.ShapeDtypeStruct((2, blocks, 8, hidden), jnp.float32),
        )
        + tuple(jax.ShapeDtypeStruct(w.shape, w.dtype) for w in weights),
        in_specs=[vmem] * len(pieces) + [pl.BlockSpec(memory_space=pltpu.HBM)] * 3,
        out_specs=(vmem,) * 6,
        scratch_shapes=[pltpu.SemaphoreType.DMA((3,))],
        compiler_params=pltpu.CompilerParams(vmem_limit_bytes=VMEM_LIMIT),
        cost_estimate=pl.CostEstimate(
            flops=blocks * 8 * 10 * SLOTS * lanes * hidden,
            bytes_accessed=sum(4 * w.size for w in weights),
            transcendentals=0,
        ),
    )(*pieces, *weights)


def finish_kernel(n_pieces, *refs):
    pieces, weights = refs[:n_pieces], refs[n_pieces : n_pieces + 3]
    pt_in, c_in, parts_in, pt_out, c_out, parts_out = refs[n_pieces + 3 :]
    blocks = parts_in.shape[1]
    pt_out[: blocks * 16] = pt_in[...]
    c_out[: blocks * 8] = c_in[...]
    parts_out[:, :blocks] = parts_in[...]
    place(pieces, blocks, pt_out, c_out)
    parts_out[0, blocks:], parts_out[1, blocks:] = projections(
        pt_out[blocks * 16 :], c_out[blocks * 8 :], *weights
    )


def finish(pieces, weights, pt, cot, parts):
    blocks = parts.shape[1] + sum(p.shape[0] for p in pieces)
    lanes, hidden = pieces[0].shape[2], weights[0].shape[1]
    vmem = pl.BlockSpec(memory_space=pltpu.VMEM)
    return pl.pallas_call(
        functools.partial(finish_kernel, len(pieces)),
        out_shape=(
            jax.ShapeDtypeStruct((blocks * 16, lanes), jnp.bfloat16),
            jax.ShapeDtypeStruct((blocks * 8, lanes), jnp.bfloat16),
            jax.ShapeDtypeStruct((2, blocks, 8, hidden), jnp.float32),
        ),
        in_specs=[vmem] * (len(pieces) + 6),
        out_specs=(vmem,) * 3,
        compiler_params=pltpu.CompilerParams(vmem_limit_bytes=VMEM_LIMIT),
    )(*pieces, *weights, pt, cot, parts)


def factors(gate, up, tgate, tup, dact):
    sig = 1.0 / (1.0 + jnp.exp(-gate))
    act = gate * sig
    first = sig * (1.0 + gate * (1.0 - sig))
    second = sig * (1.0 - sig) * (2.0 + gate * (1.0 - 2.0 * sig))
    dgate = dact * up * first
    dup = dact * act
    tdgate = dact * (tup * first + up * second * tgate)
    tdup = dact * first * tgate
    tact = tgate * first * up + act * tup
    return (dgate, dup, tdgate, tdup, tact)


def by_slot(x):
    rows = x.size // x.shape[-1]
    return jnp.concatenate(
        [only_slot(x, s).reshape(rows, x.shape[-1]) for s in range(SLOTS)], axis=1
    ).astype(jnp.bfloat16)


def middle_kernel(n_parts, groups, *refs):
    parts, (gate_w, up_w) = refs[:n_parts], refs[n_parts : n_parts + 2]
    factor_out, tact_out = refs[n_parts + 2 : n_parts + 4]
    own_out, others_out = refs[n_parts + 4], refs[n_parts + 5 :]
    packed, dact = (sum(p[k] for p in parts[1:]) + parts[0][k] for k in range(2))
    gate, up, tgate, tup = (over_slots(only_slot(packed, s)) for s in range(SLOTS))
    dgate, dup, tdgate, tdup, tact = factors(gate, up, tgate, tup, dact)
    blocks, _, hidden = gate.shape
    second = jnp.concatenate([tdgate, tdup], axis=2)
    pair = jnp.stack([second, jnp.concatenate([dgate, dup], axis=2)], axis=1)
    factor_out[...] = by_slot(pair)
    tact_out[...] = by_slot(tact)
    right = jnp.concatenate(
        [rows_for_slot(w[...], s) for s in range(SLOTS) for w in (gate_w, up_w)], axis=1
    )
    hvp = lax.dot_general(
        by_slot(second),
        right,
        (((1,), (1,)), ((), ())),
        preferred_element_type=jnp.float32,
    )
    hvp = hvp.reshape(blocks, 8, hvp.shape[1])
    inner = blocks // groups
    own_out[...] = hvp[:inner]
    early = inner + groups - 1
    for g, out in enumerate(others_out):
        at = early + g * (inner - 1)
        out[0] = hvp[inner + g].astype(out.dtype)
        out[1:] = hvp[at : at + inner - 1].astype(out.dtype)


def middle(parts, gate_w, up_w, groups):
    _, blocks, _, hidden = parts[0].shape
    lanes = gate_w.shape[0] // SLOTS
    vmem = pl.BlockSpec(memory_space=pltpu.VMEM)
    group = (blocks // groups, 8, lanes)
    return pl.pallas_call(
        functools.partial(middle_kernel, len(parts), groups),
        out_shape=(
            jax.ShapeDtypeStruct((blocks * 16, SLOTS * 2 * hidden), jnp.bfloat16),
            jax.ShapeDtypeStruct((blocks * 8, SLOTS * hidden), jnp.bfloat16),
            jax.ShapeDtypeStruct(group, jnp.float32),
        )
        + (jax.ShapeDtypeStruct(group, jnp.bfloat16),) * (groups - 1),
        in_specs=[vmem] * (len(parts) + 2),
        out_specs=(vmem,) * (groups + 2),
        compiler_params=pltpu.CompilerParams(vmem_limit_bytes=VMEM_LIMIT),
    )(*parts, gate_w, up_w)


def contract_first(left, right):
    return lax.dot_general(
        left, right, (((0,), (0,)), ((), ())), preferred_element_type=jnp.float32
    )


def up_grads_kernel(pt, factor, gate_out, up_out):
    hidden = gate_out.shape[1]
    for m in range(pt.shape[1] // LANES):
        both = contract_first(pt[:, m * LANES : (m + 1) * LANES], factor[...])
        for s in range(SLOTS):
            at = (m * SLOTS + s) * LANES
            half = 2 * s * hidden
            gate_out[at : at + LANES] = both[:, half : half + hidden]
            up_out[at : at + LANES] = both[:, half + hidden : half + 2 * hidden]


def up_grads(pt, factor, steps):
    rows, lanes = pt.shape
    hidden = factor.shape[1] // (2 * SLOTS)
    out = jax.ShapeDtypeStruct((SLOTS * lanes, hidden), jnp.float32)
    spec = pl.BlockSpec((SLOTS * lanes // steps, hidden), lambda m: (m, 0))
    return pl.pallas_call(
        up_grads_kernel,
        grid=(steps,),
        out_shape=(out, out),
        in_specs=[
            pl.BlockSpec((rows, lanes // steps), lambda m: (0, m)),
            pl.BlockSpec(memory_space=pltpu.VMEM),
        ],
        out_specs=(spec, spec),
        compiler_params=pltpu.CompilerParams(vmem_limit_bytes=VMEM_LIMIT),
        cost_estimate=pl.CostEstimate(
            flops=2 * pt.size * factor.shape[1],
            bytes_accessed=8 * SLOTS * lanes * hidden,
            transcendentals=0,
        ),
    )(pt, factor)


def down_grad_kernel(cot, tact, down_out):
    hidden = down_out.shape[0]
    for m in range(cot.shape[1] // LANES):
        tiles = contract_first(tact[...], cot[:, m * LANES : (m + 1) * LANES])
        for s in range(SLOTS):
            at = (m * SLOTS + s) * LANES
            down_out[:, at : at + LANES] = tiles[s * hidden : (s + 1) * hidden]


def down_grad(cot, tact, steps):
    rows, lanes = cot.shape
    hidden = tact.shape[1] // SLOTS
    return pl.pallas_call(
        down_grad_kernel,
        grid=(steps,),
        out_shape=jax.ShapeDtypeStruct((hidden, SLOTS * lanes), jnp.float32),
        in_specs=[
            pl.BlockSpec((rows, lanes // steps), lambda m: (0, m)),
            pl.BlockSpec(memory_space=pltpu.VMEM),
        ],
        out_specs=pl.BlockSpec((hidden, SLOTS * lanes // steps), lambda m: (0, m)),
        compiler_params=pltpu.CompilerParams(vmem_limit_bytes=VMEM_LIMIT),
        cost_estimate=pl.CostEstimate(
            flops=2 * cot.size * tact.shape[1],
            bytes_accessed=4 * SLOTS * lanes * hidden,
            transcendentals=0,
        ),
    )(cot, tact)


def solution(mesh):
    wide, narrow = mesh.shape["wide"], mesh.shape["narrow"]

    def local(primal_in, tangent_in, cotangent, gate_weight, up_weight, down_weight):
        weights = (gate_weight, up_weight, down_weight)
        early, late = gather_blocks(
            fold(primal_in, tangent_in, cotangent), "wide", wide
        )
        *first, gate_weight, up_weight, down_weight = begin(early, weights)
        weights = (gate_weight, up_weight, down_weight)
        pt, cot, part = finish(late, weights, *first)
        parts = [part]
        for shift in range(1, narrow):
            pairs = [(i, (i + shift) % narrow) for i in range(narrow)]
            parts.append(lax.ppermute(part, "narrow", pairs))
        groups = levels_of(wide)[-1][1]
        factor, tact, *hvp = middle(parts, gate_weight, up_weight, groups)
        total = scatter_sum(hvp, "wide", wide)
        input_hvp = unfold(total[0].astype(jnp.bfloat16))
        steps = max(1, pt.shape[1] // (2 * LANES))
        gate_grad, up_grad = up_grads(pt, factor, steps)
        return (input_hvp, gate_grad, up_grad, down_grad(cot, tact, steps))

    return jax.shard_map(
        local,
        mesh=mesh,
        in_specs=(
            P("wide", "narrow"),
            P("wide", "narrow"),
            P("wide", "narrow"),
            P("narrow", "wide"),
            P("narrow", "wide"),
            P("wide", "narrow"),
        ),
        out_specs=(
            P("wide", "narrow"),
            P("narrow", "wide"),
            P("narrow", "wide"),
            P("wide", "narrow"),
        ),
        check_vma=False,
    )
```

```python
import functools

import jax
import jax.numpy as jnp
from jax import lax
from jax.experimental import pallas as pl
from jax.experimental.pallas import tpu as pltpu
from jax.sharding import PartitionSpec as P

SLOTS = 4
LANES = 128
VMEM_LIMIT = 24 * 2**20


def levels_of(size):
    levels, stride = [], 1
    while stride < size:
        rest = size // stride
        radix = next(r for r in (4, 2, 3, 5, 7, rest) if rest % r == 0)
        levels.append((stride, radix))
        stride *= radix
    return levels[::-1]


def partner(index, stride, radix, offset):
    digit = index // stride % radix
    if radix & (radix - 1) == 0:
        other = digit ^ offset
    else:
        other = (digit + offset) % radix
    return index + (other - digit) * stride


def fetch(value, axis, size, level, offset):
    pairs = [(partner(i, *level, offset), i) for i in range(size)]
    return lax.ppermute(value, axis, pairs)


def deliver(value, axis, size, level, offset):
    pairs = [(i, partner(i, *level, offset)) for i in range(size)]
    return lax.ppermute(value, axis, pairs)


def after(value, earlier):
    return lax.optimization_barrier((value, earlier))[0]


def offsets_of(radix):
    return range(radix - 1, 0, -1)


def gather_blocks(own, axis, size):
    early, late = [own], []
    for level in levels_of(size):
        early, late = early + late, []
        rest = early[1:]
        offsets = offsets_of(level[1])
        held = jnp.concatenate(rest) if rest else None
        mine = [fetch(own, axis, size, level, o) for o in offsets]
        if rest:
            late = [
                fetch(after(held, came), axis, size, level, o)
                for o, came in zip(offsets, mine)
            ]
            early = [own, held]
            if level[0] > 1:
                late = [x for pair in zip(mine, late) for x in pair]
                mine = []
        early = early + mine
    return early, late


def scatter_sum(groups, axis, size, beside):
    for level in levels_of(size)[::-1]:
        if len(groups) == 1:
            groups = jnp.split(after(groups[0], beside), level[1])
        came = [
            deliver(group.astype(jnp.bfloat16), axis, size, level, o)
            for o, group in zip(offsets_of(level[1]), groups[1:])
        ]
        total = groups[0]
        for block in came[::-1]:
            total = total + block.astype(jnp.float32)
        groups = [total]
    return groups[0]


def fold(*rows):
    stacked = lax.optimization_barrier(jnp.stack(rows))
    count, tokens, width = stacked.shape
    split = stacked.reshape(count, tokens, width // (SLOTS * LANES), SLOTS, LANES)
    return split.transpose(0, 3, 1, 2, 4).reshape(1, -1, width // SLOTS)


def unfold(rows):
    tokens = rows.shape[0] // SLOTS
    split = rows.reshape(SLOTS, tokens, rows.shape[1] // LANES, LANES)
    return split.transpose(1, 2, 0, 3).reshape(tokens, rows.shape[1] * SLOTS)


def slot_of(shape, axis):
    return lax.broadcasted_iota(jnp.int32, shape, axis) // 2


def rows_for_slot(weight, slot):
    height, width = weight.shape
    split = weight.reshape(height // (SLOTS * LANES), SLOTS, LANES, width)
    return split[:, slot].reshape(height // SLOTS, width)


def over_slots(x):
    axis = x.ndim - 2
    x = x + pltpu.roll(x, 4, axis)
    return x + pltpu.roll(x, 2, axis)


def pick_slots(parts):
    slot = slot_of(parts[0].shape, parts[0].ndim - 2)
    result = parts[0]
    for s in range(1, SLOTS):
        result = jnp.where(slot == s, parts[s], result)
    return result


def only_slot(x, s):
    return jnp.where(slot_of(x.shape, x.ndim - 2) == s, x, 0.0)


def place(pieces, at, pt_out, c_out):
    for piece in pieces:
        for i in range(piece.shape[0]):
            pt_out[at * 16 : at * 16 + 16] = piece[i, 0:16]
            c_out[at * 8 : at * 8 + 8] = piece[i, 16:24]
            at += 1


def projections(pt, cot, gate_w, up_w, down_w):
    blocks, hidden = cot.shape[0] // 8, gate_w.shape[1]
    acts, dacts = [], []
    for s in range(SLOTS):
        weights = jnp.concatenate(
            [rows_for_slot(gate_w[...], s), rows_for_slot(up_w[...], s)], axis=1
        )
        acts.append(
            jnp.dot(pt, weights, preferred_element_type=jnp.float32).reshape(
                2 * blocks, 8, 2 * hidden
            )
        )
        columns = [
            down_w[:, j * LANES : (j + 1) * LANES]
            for j in range(s, down_w.shape[1] // LANES, SLOTS)
        ]
        dacts.append(
            lax.dot_general(
                cot,
                jnp.concatenate(columns, axis=1),
                (((1,), (1,)), ((), ())),
                preferred_element_type=jnp.float32,
            ).reshape(blocks, 8, hidden)
        )
    act = over_slots(pick_slots(acts)).reshape(blocks, 2, 8, 2 * hidden)
    packed = pick_slots(
        [
            act[:, 0, :, :hidden],
            act[:, 0, :, hidden:],
            act[:, 1, :, :hidden],
            act[:, 1, :, hidden:],
        ]
    )
    return packed, over_slots(pick_slots(dacts))


def begin_kernel(n_pieces, *refs):
    pieces, weights = refs[:n_pieces], refs[n_pieces : n_pieces + 3]
    pt_out, c_out, parts_out, *held, sems = refs[n_pieces + 3 :]
    copies = [
        pltpu.make_async_copy(w, h, sems.at[k])
        for k, (w, h) in enumerate(zip(weights, held))
    ]
    for copy in copies:
        copy.start()
    place(pieces, 0, pt_out, c_out)
    for copy in copies:
        copy.wait()
    parts_out[0], parts_out[1] = projections(pt_out[...], c_out[...], *held)


def begin(pieces, weights):
    blocks = sum(p.shape[0] for p in pieces)
    lanes, hidden = pieces[0].shape[2], weights[0].shape[1]
    vmem = pl.BlockSpec(memory_space=pltpu.VMEM)
    return pl.pallas_call(
        functools.partial(begin_kernel, len(pieces)),
        out_shape=(
            jax.ShapeDtypeStruct((blocks * 16, lanes), jnp.bfloat16),
            jax.ShapeDtypeStruct((blocks * 8, lanes), jnp.bfloat16),
            jax.ShapeDtypeStruct((2, blocks, 8, hidden), jnp.float32),
        )
        + tuple(jax.ShapeDtypeStruct(w.shape, w.dtype) for w in weights),
        in_specs=[vmem] * len(pieces) + [pl.BlockSpec(memory_space=pltpu.HBM)] * 3,
        out_specs=(vmem,) * 6,
        scratch_shapes=[pltpu.SemaphoreType.DMA((3,))],
        compiler_params=pltpu.CompilerParams(vmem_limit_bytes=VMEM_LIMIT),
        cost_estimate=pl.CostEstimate(
            flops=blocks * 8 * 10 * SLOTS * lanes * hidden,
            bytes_accessed=sum(4 * w.size for w in weights),
            transcendentals=0,
        ),
    )(*pieces, *weights)


def finish_kernel(n_pieces, *refs):
    pieces, weights = refs[:n_pieces], refs[n_pieces : n_pieces + 3]
    pt_in, c_in, parts_in, pt_out, c_out, parts_out = refs[n_pieces + 3 :]
    blocks = parts_in.shape[1]
    pt_out[: blocks * 16] = pt_in[...]
    c_out[: blocks * 8] = c_in[...]
    parts_out[:, :blocks] = parts_in[...]
    place(pieces, blocks, pt_out, c_out)
    parts_out[0, blocks:], parts_out[1, blocks:] = projections(
        pt_out[blocks * 16 :], c_out[blocks * 8 :], *weights
    )


def finish(pieces, weights, pt, cot, parts):
    blocks = parts.shape[1] + sum(p.shape[0] for p in pieces)
    lanes, hidden = pieces[0].shape[2], weights[0].shape[1]
    vmem = pl.BlockSpec(memory_space=pltpu.VMEM)
    return pl.pallas_call(
        functools.partial(finish_kernel, len(pieces)),
        out_shape=(
            jax.ShapeDtypeStruct((blocks * 16, lanes), jnp.bfloat16),
            jax.ShapeDtypeStruct((blocks * 8, lanes), jnp.bfloat16),
            jax.ShapeDtypeStruct((2, blocks, 8, hidden), jnp.float32),
        ),
        in_specs=[vmem] * (len(pieces) + 6),
        out_specs=(vmem,) * 3,
        compiler_params=pltpu.CompilerParams(vmem_limit_bytes=VMEM_LIMIT),
    )(*pieces, *weights, pt, cot, parts)


def factors(gate, up, tgate, tup, dact):
    sig = 1.0 / (1.0 + jnp.exp(-gate))
    act = gate * sig
    first = sig * (1.0 + gate * (1.0 - sig))
    second = sig * (1.0 - sig) * (2.0 + gate * (1.0 - 2.0 * sig))
    dgate = dact * up * first
    dup = dact * act
    tdgate = dact * (tup * first + up * second * tgate)
    tdup = dact * first * tgate
    tact = tgate * first * up + act * tup
    return (dgate, dup, tdgate, tdup, tact)


def by_slot(x):
    rows = x.size // x.shape[-1]
    return jnp.concatenate(
        [only_slot(x, s).reshape(rows, x.shape[-1]) for s in range(SLOTS)], axis=1
    ).astype(jnp.bfloat16)


def middle_kernel(n_parts, groups, *refs):
    parts, (gate_w, up_w) = refs[:n_parts], refs[n_parts : n_parts + 2]
    factor_out, tact_out = refs[n_parts + 2 : n_parts + 4]
    own_out, others_out = refs[n_parts + 4], refs[n_parts + 5 :]
    packed, dact = (sum(p[k] for p in parts[1:]) + parts[0][k] for k in range(2))
    gate, up, tgate, tup = (over_slots(only_slot(packed, s)) for s in range(SLOTS))
    dgate, dup, tdgate, tdup, tact = factors(gate, up, tgate, tup, dact)
    blocks, _, hidden = gate.shape
    second = jnp.concatenate([tdgate, tdup], axis=2)
    pair = jnp.stack([second, jnp.concatenate([dgate, dup], axis=2)], axis=1)
    factor_out[...] = by_slot(pair)
    tact_out[...] = by_slot(tact)
    right = jnp.concatenate(
        [rows_for_slot(w[...], s) for s in range(SLOTS) for w in (gate_w, up_w)], axis=1
    )
    hvp = lax.dot_general(
        by_slot(second),
        right,
        (((1,), (1,)), ((), ())),
        preferred_element_type=jnp.float32,
    )
    hvp = hvp.reshape(blocks, 8, hvp.shape[1])
    inner = blocks // groups
    own_out[...] = hvp[:inner]
    early = inner + groups - 1
    for g, out in enumerate(others_out):
        at = early + g * (inner - 1)
        out[0] = hvp[inner + g].astype(out.dtype)
        out[1:] = hvp[at : at + inner - 1].astype(out.dtype)


def middle(parts, gate_w, up_w, groups):
    _, blocks, _, hidden = parts[0].shape
    lanes = gate_w.shape[0] // SLOTS
    vmem = pl.BlockSpec(memory_space=pltpu.VMEM)
    group = (blocks // groups, 8, lanes)
    return pl.pallas_call(
        functools.partial(middle_kernel, len(parts), groups),
        out_shape=(
            jax.ShapeDtypeStruct((blocks * 16, SLOTS * 2 * hidden), jnp.bfloat16),
            jax.ShapeDtypeStruct((blocks * 8, SLOTS * hidden), jnp.bfloat16),
            jax.ShapeDtypeStruct(group, jnp.float32),
        )
        + (jax.ShapeDtypeStruct(group, jnp.bfloat16),) * (groups - 1),
        in_specs=[vmem] * (len(parts) + 2),
        out_specs=(vmem,) * (groups + 2),
        compiler_params=pltpu.CompilerParams(vmem_limit_bytes=VMEM_LIMIT),
    )(*parts, gate_w, up_w)


def contract_first(left, right):
    return lax.dot_general(
        left, right, (((0,), (0,)), ((), ())), preferred_element_type=jnp.float32
    )


def up_grads_kernel(pt, factor, gate_out, up_out):
    hidden = gate_out.shape[1]
    for m in range(pt.shape[1] // LANES):
        both = contract_first(pt[:, m * LANES : (m + 1) * LANES], factor[...])
        for s in range(SLOTS):
            at = (m * SLOTS + s) * LANES
            half = 2 * s * hidden
            gate_out[at : at + LANES] = both[:, half : half + hidden]
            up_out[at : at + LANES] = both[:, half + hidden : half + 2 * hidden]


def up_grads(pt, factor, steps):
    rows, lanes = pt.shape
    hidden = factor.shape[1] // (2 * SLOTS)
    out = jax.ShapeDtypeStruct((SLOTS * lanes, hidden), jnp.float32)
    spec = pl.BlockSpec((SLOTS * lanes // steps, hidden), lambda m: (m, 0))
    return pl.pallas_call(
        up_grads_kernel,
        grid=(steps,),
        out_shape=(out, out),
        in_specs=[
            pl.BlockSpec((rows, lanes // steps), lambda m: (0, m)),
            pl.BlockSpec(memory_space=pltpu.VMEM),
        ],
        out_specs=(spec, spec),
        compiler_params=pltpu.CompilerParams(vmem_limit_bytes=VMEM_LIMIT),
        cost_estimate=pl.CostEstimate(
            flops=2 * pt.size * factor.shape[1],
            bytes_accessed=8 * SLOTS * lanes * hidden,
            transcendentals=0,
        ),
    )(pt, factor)


def down_grad_kernel(cot, tact, down_out):
    hidden = down_out.shape[0]
    for m in range(cot.shape[1] // LANES):
        tiles = contract_first(tact[...], cot[:, m * LANES : (m + 1) * LANES])
        for s in range(SLOTS):
            at = (m * SLOTS + s) * LANES
            down_out[:, at : at + LANES] = tiles[s * hidden : (s + 1) * hidden]


def down_grad(cot, tact, steps):
    rows, lanes = cot.shape
    hidden = tact.shape[1] // SLOTS
    return pl.pallas_call(
        down_grad_kernel,
        grid=(steps,),
        out_shape=jax.ShapeDtypeStruct((hidden, SLOTS * lanes), jnp.float32),
        in_specs=[
            pl.BlockSpec((rows, lanes // steps), lambda m: (0, m)),
            pl.BlockSpec(memory_space=pltpu.VMEM),
        ],
        out_specs=pl.BlockSpec((hidden, SLOTS * lanes // steps), lambda m: (0, m)),
        compiler_params=pltpu.CompilerParams(vmem_limit_bytes=VMEM_LIMIT),
        cost_estimate=pl.CostEstimate(
            flops=2 * cot.size * tact.shape[1],
            bytes_accessed=4 * SLOTS * lanes * hidden,
            transcendentals=0,
        ),
    )(cot, tact)


def solution(mesh):
    wide, narrow = mesh.shape["wide"], mesh.shape["narrow"]

    def local(primal_in, tangent_in, cotangent, gate_weight, up_weight, down_weight):
        weights = (gate_weight, up_weight, down_weight)
        early, late = gather_blocks(
            fold(primal_in, tangent_in, cotangent), "wide", wide
        )
        *first, gate_weight, up_weight, down_weight = begin(early, weights)
        weights = (gate_weight, up_weight, down_weight)
        pt, cot, part = finish(late, weights, *first)
        parts = [part]
        for shift in range(1, narrow):
            pairs = [(i, (i + shift) % narrow) for i in range(narrow)]
            parts.append(lax.ppermute(part, "narrow", pairs))
        groups = levels_of(wide)[-1][1]
        factor, tact, *hvp = middle(parts, gate_weight, up_weight, groups)
        steps = max(1, pt.shape[1] // (2 * LANES))
        gate_grad, up_grad = up_grads(pt, factor, steps)
        total = scatter_sum(hvp, "wide", wide, gate_grad)
        input_hvp = unfold(total[0].astype(jnp.bfloat16))
        return (input_hvp, gate_grad, up_grad, down_grad(cot, tact, steps))

    return jax.shard_map(
        local,
        mesh=mesh,
        in_specs=(
            P("wide", "narrow"),
            P("wide", "narrow"),
            P("wide", "narrow"),
            P("narrow", "wide"),
            P("narrow", "wide"),
            P("wide", "narrow"),
        ),
        out_specs=(
            P("wide", "narrow"),
            P("narrow", "wide"),
            P("narrow", "wide"),
            P("wide", "narrow"),
        ),
        check_vma=False,
    )
```

```python
import functools

import jax
import jax.numpy as jnp
from jax import lax
from jax.experimental import pallas as pl
from jax.experimental.pallas import tpu as pltpu
from jax.sharding import PartitionSpec as P

SLOTS = 4
LANES = 128
VMEM_LIMIT = 24 * 2**20


def levels_of(size):
    levels, stride = [], 1
    while stride < size:
        rest = size // stride
        radix = next(r for r in (4, 2, 3, 5, 7, rest) if rest % r == 0)
        levels.append((stride, radix))
        stride *= radix
    return levels[::-1]


def partner(index, stride, radix, offset):
    digit = index // stride % radix
    if radix & (radix - 1) == 0:
        other = digit ^ offset
    else:
        other = (digit + offset) % radix
    return index + (other - digit) * stride


def fetch(value, axis, size, level, offset):
    pairs = [(partner(i, *level, offset), i) for i in range(size)]
    return lax.ppermute(value, axis, pairs)


def deliver(value, axis, size, level, offset):
    pairs = [(i, partner(i, *level, offset)) for i in range(size)]
    return lax.ppermute(value, axis, pairs)


def after(value, earlier):
    return lax.optimization_barrier((value, earlier))[0]


def offsets_of(radix):
    return range(radix - 1, 0, -1)


def gather_blocks(own, axis, size):
    early, late, count = [(own, [0])], [], 1
    before = None
    for level in levels_of(size):
        rest = early[1:] + late
        offsets = list(offsets_of(level[1]))
        slots = {o: count * (k + 1) for k, o in enumerate(offsets)}
        starts = offsets[::-1] if rest else offsets
        mine = {o: fetch(own, axis, size, level, o) for o in starts}
        late = [(mine[o], [slots[o]]) for o in starts]
        early = [(own, [0])]
        if rest:
            held = join(rest)
            step, near = before
            far = join([piece for piece in rest if piece[1] != [near]])
            early, late = early + [held] + late, []
            for o, first in zip(offsets, starts[:1] * 2 + starts[1:]):
                part, ids = far if o & (o - 1) else held
                block = fetch(after(part, mine[first]), axis, size, level, o)
                late.append((block, [slots[o] + i for i in ids]))
            for o in offsets:
                if o & (o - 1):
                    block = fetch(mine[o], axis, size, step, 1)
                    late.append((block, [slots[o] + near]))
        before = level, slots[1]
        count *= level[1]
    pieces = early + late
    ids = sum((ids for _, ids in pieces), [])
    order = [ids.index(k) for k in range(count)]
    return [block for block, _ in early], [block for block, _ in late], order


def join(pieces):
    blocks = jnp.concatenate([block for block, _ in pieces])
    return blocks, sum((ids for _, ids in pieces), [])


def scatter_sum(groups, axis, size, beside):
    for level in levels_of(size)[::-1]:
        if len(groups) == 1:
            groups = jnp.split(after(groups[0], beside), level[1])
        came = [
            deliver(group.astype(jnp.bfloat16), axis, size, level, o)
            for o, group in zip(offsets_of(level[1]), groups[1:])
        ]
        total = groups[0]
        for block in came[::-1]:
            total = total + block.astype(jnp.float32)
        groups = [total]
    return groups[0]


def fold(*rows):
    stacked = lax.optimization_barrier(jnp.stack(rows))
    count, tokens, width = stacked.shape
    split = stacked.reshape(count, tokens, width // (SLOTS * LANES), SLOTS, LANES)
    return split.transpose(0, 3, 1, 2, 4).reshape(1, -1, width // SLOTS)


def unfold(rows):
    tokens = rows.shape[0] // SLOTS
    split = rows.reshape(SLOTS, tokens, rows.shape[1] // LANES, LANES)
    return split.transpose(1, 2, 0, 3).reshape(tokens, rows.shape[1] * SLOTS)


def slot_of(shape, axis):
    return lax.broadcasted_iota(jnp.int32, shape, axis) // 2


def rows_for_slot(weight, slot):
    height, width = weight.shape
    split = weight.reshape(height // (SLOTS * LANES), SLOTS, LANES, width)
    return split[:, slot].reshape(height // SLOTS, width)


def over_slots(x):
    axis = x.ndim - 2
    x = x + pltpu.roll(x, 4, axis)
    return x + pltpu.roll(x, 2, axis)


def pick_slots(parts):
    slot = slot_of(parts[0].shape, parts[0].ndim - 2)
    result = parts[0]
    for s in range(1, SLOTS):
        result = jnp.where(slot == s, parts[s], result)
    return result


def only_slot(x, s):
    return jnp.where(slot_of(x.shape, x.ndim - 2) == s, x, 0.0)


def place(pieces, at, pt_out, c_out):
    for piece in pieces:
        for i in range(piece.shape[0]):
            pt_out[at * 16 : at * 16 + 16] = piece[i, 0:16]
            c_out[at * 8 : at * 8 + 8] = piece[i, 16:24]
            at += 1


def projections(pt, cot, gate_w, up_w, down_w):
    blocks, hidden = cot.shape[0] // 8, gate_w.shape[1]
    acts, dacts = [], []
    for s in range(SLOTS):
        weights = jnp.concatenate(
            [rows_for_slot(gate_w[...], s), rows_for_slot(up_w[...], s)], axis=1
        )
        acts.append(
            jnp.dot(pt, weights, preferred_element_type=jnp.float32).reshape(
                2 * blocks, 8, 2 * hidden
            )
        )
        columns = [
            down_w[:, j * LANES : (j + 1) * LANES]
            for j in range(s, down_w.shape[1] // LANES, SLOTS)
        ]
        dacts.append(
            lax.dot_general(
                cot,
                jnp.concatenate(columns, axis=1),
                (((1,), (1,)), ((), ())),
                preferred_element_type=jnp.float32,
            ).reshape(blocks, 8, hidden)
        )
    act = over_slots(pick_slots(acts)).reshape(blocks, 2, 8, 2 * hidden)
    packed = pick_slots(
        [
            act[:, 0, :, :hidden],
            act[:, 0, :, hidden:],
            act[:, 1, :, :hidden],
            act[:, 1, :, hidden:],
        ]
    )
    return packed, over_slots(pick_slots(dacts))


def begin_kernel(n_pieces, *refs):
    pieces, weights = refs[:n_pieces], refs[n_pieces : n_pieces + 3]
    pt_out, c_out, parts_out, *held, sems = refs[n_pieces + 3 :]
    copies = [
        pltpu.make_async_copy(w, h, sems.at[k])
        for k, (w, h) in enumerate(zip(weights, held))
    ]
    for copy in copies:
        copy.start()
    place(pieces, 0, pt_out, c_out)
    for copy in copies:
        copy.wait()
    parts_out[0], parts_out[1] = projections(pt_out[...], c_out[...], *held)


def begin(pieces, weights):
    blocks = sum(p.shape[0] for p in pieces)
    lanes, hidden = pieces[0].shape[2], weights[0].shape[1]
    vmem = pl.BlockSpec(memory_space=pltpu.VMEM)
    return pl.pallas_call(
        functools.partial(begin_kernel, len(pieces)),
        out_shape=(
            jax.ShapeDtypeStruct((blocks * 16, lanes), jnp.bfloat16),
            jax.ShapeDtypeStruct((blocks * 8, lanes), jnp.bfloat16),
            jax.ShapeDtypeStruct((2, blocks, 8, hidden), jnp.float32),
        )
        + tuple(jax.ShapeDtypeStruct(w.shape, w.dtype) for w in weights),
        in_specs=[vmem] * len(pieces) + [pl.BlockSpec(memory_space=pltpu.HBM)] * 3,
        out_specs=(vmem,) * 6,
        scratch_shapes=[pltpu.SemaphoreType.DMA((3,))],
        compiler_params=pltpu.CompilerParams(vmem_limit_bytes=50 * 2**20),
        cost_estimate=pl.CostEstimate(
            flops=blocks * 8 * 10 * SLOTS * lanes * hidden,
            bytes_accessed=sum(4 * w.size for w in weights),
            transcendentals=0,
        ),
    )(*pieces, *weights)


def finish_kernel(n_pieces, *refs):
    pieces, weights = refs[:n_pieces], refs[n_pieces : n_pieces + 3]
    pt_in, c_in, parts_in, pt_out, c_out, parts_out = refs[n_pieces + 3 :]
    blocks = parts_in.shape[1]
    pt_out[: blocks * 16] = pt_in[...]
    c_out[: blocks * 8] = c_in[...]
    parts_out[:, :blocks] = parts_in[...]
    place(pieces, blocks, pt_out, c_out)
    parts_out[0, blocks:], parts_out[1, blocks:] = projections(
        pt_out[blocks * 16 :], c_out[blocks * 8 :], *weights
    )


def finish(pieces, weights, pt, cot, parts):
    blocks = parts.shape[1] + sum(p.shape[0] for p in pieces)
    lanes, hidden = pieces[0].shape[2], weights[0].shape[1]
    vmem = pl.BlockSpec(memory_space=pltpu.VMEM)
    return pl.pallas_call(
        functools.partial(finish_kernel, len(pieces)),
        out_shape=(
            jax.ShapeDtypeStruct((blocks * 16, lanes), jnp.bfloat16),
            jax.ShapeDtypeStruct((blocks * 8, lanes), jnp.bfloat16),
            jax.ShapeDtypeStruct((2, blocks, 8, hidden), jnp.float32),
        ),
        in_specs=[vmem] * (len(pieces) + 6),
        out_specs=(vmem,) * 3,
        compiler_params=pltpu.CompilerParams(vmem_limit_bytes=VMEM_LIMIT),
    )(*pieces, *weights, pt, cot, parts)


def factors(gate, up, tgate, tup, dact):
    sig = 1.0 / (1.0 + jnp.exp(-gate))
    act = gate * sig
    first = sig * (1.0 + gate * (1.0 - sig))
    second = sig * (1.0 - sig) * (2.0 + gate * (1.0 - 2.0 * sig))
    dgate = dact * up * first
    dup = dact * act
    tdgate = dact * (tup * first + up * second * tgate)
    tdup = dact * first * tgate
    tact = tgate * first * up + act * tup
    return (dgate, dup, tdgate, tdup, tact)


def by_slot(x):
    rows = x.size // x.shape[-1]
    return jnp.concatenate(
        [only_slot(x, s).reshape(rows, x.shape[-1]) for s in range(SLOTS)], axis=1
    ).astype(jnp.bfloat16)


def middle_kernel(n_parts, groups, order, *refs):
    parts, (gate_w, up_w) = refs[:n_parts], refs[n_parts : n_parts + 2]
    factor_out, tact_out = refs[n_parts + 2 : n_parts + 4]
    own_out, others_out = refs[n_parts + 4], refs[n_parts + 5 :]
    packed, dact = (sum(p[k] for p in parts[1:]) + parts[0][k] for k in range(2))
    gate, up, tgate, tup = (over_slots(only_slot(packed, s)) for s in range(SLOTS))
    dgate, dup, tdgate, tdup, tact = factors(gate, up, tgate, tup, dact)
    blocks, _, hidden = gate.shape
    second = jnp.concatenate([tdgate, tdup], axis=2)
    pair = jnp.stack([second, jnp.concatenate([dgate, dup], axis=2)], axis=1)
    factor_out[...] = by_slot(pair)
    tact_out[...] = by_slot(tact)
    right = jnp.concatenate(
        [rows_for_slot(w[...], s) for s in range(SLOTS) for w in (gate_w, up_w)], axis=1
    )
    hvp = lax.dot_general(
        by_slot(second),
        right,
        (((1,), (1,)), ((), ())),
        preferred_element_type=jnp.float32,
    )
    hvp = hvp.reshape(blocks, 8, hvp.shape[1])
    inner = blocks // groups
    for k, at in enumerate(order):
        group, place_in = divmod(k, inner)
        out = others_out[group - 1] if group else own_out
        out[place_in] = hvp[at].astype(out.dtype)


def middle(parts, gate_w, up_w, groups, order):
    _, blocks, _, hidden = parts[0].shape
    lanes = gate_w.shape[0] // SLOTS
    vmem = pl.BlockSpec(memory_space=pltpu.VMEM)
    group = (blocks // groups, 8, lanes)
    return pl.pallas_call(
        functools.partial(middle_kernel, len(parts), groups, order),
        out_shape=(
            jax.ShapeDtypeStruct((blocks * 16, SLOTS * 2 * hidden), jnp.bfloat16),
            jax.ShapeDtypeStruct((blocks * 8, SLOTS * hidden), jnp.bfloat16),
            jax.ShapeDtypeStruct(group, jnp.float32),
        )
        + (jax.ShapeDtypeStruct(group, jnp.bfloat16),) * (groups - 1),
        in_specs=[vmem] * (len(parts) + 2),
        out_specs=(vmem,) * (groups + 2),
        compiler_params=pltpu.CompilerParams(vmem_limit_bytes=VMEM_LIMIT),
    )(*parts, gate_w, up_w)


def contract_first(left, right):
    return lax.dot_general(
        left, right, (((0,), (0,)), ((), ())), preferred_element_type=jnp.float32
    )


def up_grads_kernel(pt, factor, gate_out, up_out, gate_tiles, up_tiles, sems):
    tiles, _, hidden = gate_tiles.shape
    copies = []
    for m in range(tiles):
        both = contract_first(pt[:, m * LANES : (m + 1) * LANES], factor[...])
        for s in range(SLOTS):
            at, half = slice(s * LANES, (s + 1) * LANES), 2 * s * hidden
            gate_tiles[m, at] = both[:, half : half + hidden]
            up_tiles[m, at] = both[:, half + hidden : half + 2 * hidden]
        rows = slice(m * SLOTS * LANES, (m + 1) * SLOTS * LANES)
        for k, (tile, out) in enumerate(((gate_tiles, gate_out), (up_tiles, up_out))):
            copies.append(pltpu.make_async_copy(tile.at[m], out.at[rows], sems.at[m, k]))
            copies[-1].start()
    for copy in copies:
        copy.wait()


def up_grads(pt, factor):
    rows, lanes = pt.shape
    tiles, hidden = lanes // LANES, factor.shape[1] // (2 * SLOTS)
    out = jax.ShapeDtypeStruct((SLOTS * lanes, hidden), jnp.float32)
    vmem = pl.BlockSpec(memory_space=pltpu.VMEM)
    return pl.pallas_call(
        up_grads_kernel,
        out_shape=(out, out),
        in_specs=[vmem] * 2,
        out_specs=(pl.BlockSpec(memory_space=pltpu.HBM),) * 2,
        scratch_shapes=[
            pltpu.VMEM((tiles, SLOTS * LANES, hidden), jnp.float32),
            pltpu.VMEM((tiles, SLOTS * LANES, hidden), jnp.float32),
            pltpu.SemaphoreType.DMA((tiles, 2)),
        ],
        compiler_params=pltpu.CompilerParams(vmem_limit_bytes=VMEM_LIMIT),
        cost_estimate=pl.CostEstimate(
            flops=2 * pt.size * factor.shape[1],
            bytes_accessed=8 * SLOTS * lanes * hidden,
            transcendentals=0,
        ),
    )(pt, factor)


def down_grad_kernel(cot, tact, down_out, down_tiles, sems):
    tiles, hidden, _ = down_tiles.shape
    copies = []
    for m in range(tiles):
        down = contract_first(tact[...], cot[:, m * LANES : (m + 1) * LANES])
        for s in range(SLOTS):
            at = slice(s * LANES, (s + 1) * LANES)
            down_tiles[m, :, at] = down[s * hidden : (s + 1) * hidden]
        columns = slice(m * SLOTS * LANES, (m + 1) * SLOTS * LANES)
        copies.append(
            pltpu.make_async_copy(down_tiles.at[m], down_out.at[:, columns], sems.at[m])
        )
        copies[-1].start()
    for copy in copies:
        copy.wait()


def down_grad(cot, tact):
    lanes = cot.shape[1]
    tiles, hidden = lanes // LANES, tact.shape[1] // SLOTS
    vmem = pl.BlockSpec(memory_space=pltpu.VMEM)
    return pl.pallas_call(
        down_grad_kernel,
        out_shape=jax.ShapeDtypeStruct((hidden, SLOTS * lanes), jnp.float32),
        in_specs=[vmem] * 2,
        out_specs=pl.BlockSpec(memory_space=pltpu.HBM),
        scratch_shapes=[
            pltpu.VMEM((tiles, hidden, SLOTS * LANES), jnp.float32),
            pltpu.SemaphoreType.DMA((tiles,)),
        ],
        compiler_params=pltpu.CompilerParams(vmem_limit_bytes=VMEM_LIMIT),
        cost_estimate=pl.CostEstimate(
            flops=2 * cot.size * tact.shape[1],
            bytes_accessed=4 * SLOTS * lanes * hidden,
            transcendentals=0,
        ),
    )(cot, tact)


def solution(mesh):
    wide, narrow = mesh.shape["wide"], mesh.shape["narrow"]

    def local(primal_in, tangent_in, cotangent, gate_weight, up_weight, down_weight):
        weights = (gate_weight, up_weight, down_weight)
        early, late, order = gather_blocks(
            fold(primal_in, tangent_in, cotangent), "wide", wide
        )
        *first, gate_weight, up_weight, down_weight = begin(early, weights)
        weights = (gate_weight, up_weight, down_weight)
        pt, cot, part = finish(late, weights, *first)
        parts = [part]
        for shift in range(1, narrow):
            pairs = [(i, (i + shift) % narrow) for i in range(narrow)]
            parts.append(lax.ppermute(part, "narrow", pairs))
        groups = levels_of(wide)[-1][1]
        factor, tact, *hvp = middle(parts, gate_weight, up_weight, groups, order)
        gate_grad, up_grad = up_grads(pt, factor)
        total = scatter_sum(hvp, "wide", wide, gate_grad)
        input_hvp = unfold(total[0].astype(jnp.bfloat16))
        return (input_hvp, gate_grad, up_grad, down_grad(cot, tact))

    return jax.shard_map(
        local,
        mesh=mesh,
        in_specs=(
            P("wide", "narrow"),
            P("wide", "narrow"),
            P("wide", "narrow"),
            P("narrow", "wide"),
            P("narrow", "wide"),
            P("wide", "narrow"),
        ),
        out_specs=(
            P("wide", "narrow"),
            P("narrow", "wide"),
            P("narrow", "wide"),
            P("wide", "narrow"),
        ),
        check_vma=False,
    )
```

```python
import functools

import jax
import jax.numpy as jnp
from jax import lax
from jax.experimental import pallas as pl
from jax.experimental.pallas import tpu as pltpu
from jax.sharding import PartitionSpec as P

SLOTS = 4
LANES = 128
VMEM_LIMIT = 24 * 2**20


def levels_of(size):
    levels, stride = [], 1
    while stride < size:
        rest = size // stride
        radix = next(r for r in (4, 2, 3, 5, 7, rest) if rest % r == 0)
        levels.append((stride, radix))
        stride *= radix
    return levels[::-1]


def partner(index, stride, radix, offset):
    digit = index // stride % radix
    if radix & (radix - 1) == 0:
        other = digit ^ offset
    else:
        other = (digit + offset) % radix
    return index + (other - digit) * stride


def turned(offset, level, core):
    stride, radix = level
    if stride == 1 and radix == 4 and core % 2 and offset in (1, 2):
        return 3 - offset
    return offset


def pairs_of(sizes, level, offset):
    wide, narrow = sizes
    return [
        (i * narrow + c, partner(i, *level, turned(offset, level, c)) * narrow + c)
        for i in range(wide)
        for c in range(narrow)
    ]


def fetch(value, sizes, level, offset):
    pairs = [(there, here) for here, there in pairs_of(sizes, level, offset)]
    return lax.ppermute(value, ("wide", "narrow"), pairs)


def deliver(value, sizes, level, offset):
    return lax.ppermute(value, ("wide", "narrow"), pairs_of(sizes, level, offset))


def after(value, earlier):
    return lax.optimization_barrier((value, earlier))[0]


def offsets_of(radix):
    return range(radix - 1, 0, -1)


def aligned(order, level):
    inner = len(order) // level[1]
    slots = {o: k + 1 for k, o in enumerate(offsets_of(level[1]))} | {0: 0}
    places = [0] * len(order)
    for offset, slot in slots.items():
        other = slots[turned(offset, level, 1)]
        for k in range(inner):
            places[order[slot * inner + k]] = order[other * inner + k]
    return places


def gather_blocks(own, sizes):
    early, late, count = [(own, [0])], [], 1
    before = None
    for level in levels_of(sizes[0]):
        rest = early[1:] + late
        offsets = list(offsets_of(level[1]))
        slots = {o: count * (k + 1) for k, o in enumerate(offsets)}
        starts = offsets[::-1] if rest else offsets
        mine = {o: fetch(own, sizes, level, o) for o in starts}
        late = [(mine[o], [slots[o]]) for o in starts]
        early = [(own, [0])]
        if rest:
            held = join(rest)
            step, near = before
            far = join([piece for piece in rest if piece[1] != [near]])
            early, late = early + [held] + late, []
            for o, first in zip(offsets, starts[:1] * 2 + starts[1:]):
                part, ids = far if o & (o - 1) else held
                block = fetch(after(part, mine[first]), sizes, level, o)
                late.append((block, [slots[o] + i for i in ids]))
            for o in offsets:
                if o & (o - 1):
                    block = fetch(mine[o], sizes, step, 1)
                    late.append((block, [slots[o] + near]))
        before = level, slots[1]
        count *= level[1]
    pieces = early + late
    ids = sum((ids for _, ids in pieces), [])
    order = [ids.index(k) for k in range(count)]
    return [block for block, _ in early], [block for block, _ in late], order


def join(pieces):
    blocks = jnp.concatenate([block for block, _ in pieces])
    return blocks, sum((ids for _, ids in pieces), [])


def scatter_sum(groups, sizes, beside):
    for level in levels_of(sizes[0])[::-1]:
        if len(groups) == 1:
            groups = jnp.split(after(groups[0], beside), level[1])
        came = [
            deliver(group.astype(jnp.bfloat16), sizes, level, o)
            for o, group in zip(offsets_of(level[1]), groups[1:])
        ]
        total = groups[0]
        for block in came[::-1]:
            total = total + block.astype(jnp.float32)
        groups = [total]
    return groups[0]


def fold(*rows):
    stacked = lax.optimization_barrier(jnp.stack(rows))
    count, tokens, width = stacked.shape
    split = stacked.reshape(count, tokens, width // (SLOTS * LANES), SLOTS, LANES)
    return split.transpose(0, 3, 1, 2, 4).reshape(1, -1, width // SLOTS)


def unfold(rows):
    tokens = rows.shape[0] // SLOTS
    split = rows.reshape(SLOTS, tokens, rows.shape[1] // LANES, LANES)
    return split.transpose(1, 2, 0, 3).reshape(tokens, rows.shape[1] * SLOTS)


def slot_of(shape, axis):
    return lax.broadcasted_iota(jnp.int32, shape, axis) // 2


def rows_for_slot(weight, slot):
    height, width = weight.shape
    split = weight.reshape(height // (SLOTS * LANES), SLOTS, LANES, width)
    return split[:, slot].reshape(height // SLOTS, width)


def over_slots(x):
    axis = x.ndim - 2
    x = x + pltpu.roll(x, 4, axis)
    return x + pltpu.roll(x, 2, axis)


def pick_slots(parts):
    slot = slot_of(parts[0].shape, parts[0].ndim - 2)
    result = parts[0]
    for s in range(1, SLOTS):
        result = jnp.where(slot == s, parts[s], result)
    return result


def only_slot(x, s):
    return jnp.where(slot_of(x.shape, x.ndim - 2) == s, x, 0.0)


def place(pieces, at, pt_out, c_out):
    for piece in pieces:
        for i in range(piece.shape[0]):
            pt_out[at * 16 : at * 16 + 16] = piece[i, 0:16]
            c_out[at * 8 : at * 8 + 8] = piece[i, 16:24]
            at += 1


def projections(pt, cot, gate_w, up_w, down_w):
    blocks, hidden = cot.shape[0] // 8, gate_w.shape[1]
    acts, dacts = [], []
    for s in range(SLOTS):
        weights = jnp.concatenate(
            [rows_for_slot(gate_w[...], s), rows_for_slot(up_w[...], s)], axis=1
        )
        acts.append(
            jnp.dot(pt, weights, preferred_element_type=jnp.float32).reshape(
                2 * blocks, 8, 2 * hidden
            )
        )
        columns = [
            down_w[:, j * LANES : (j + 1) * LANES]
            for j in range(s, down_w.shape[1] // LANES, SLOTS)
        ]
        dacts.append(
            lax.dot_general(
                cot,
                jnp.concatenate(columns, axis=1),
                (((1,), (1,)), ((), ())),
                preferred_element_type=jnp.float32,
            ).reshape(blocks, 8, hidden)
        )
    act = over_slots(pick_slots(acts)).reshape(blocks, 2, 8, 2 * hidden)
    packed = pick_slots(
        [
            act[:, 0, :, :hidden],
            act[:, 0, :, hidden:],
            act[:, 1, :, :hidden],
            act[:, 1, :, hidden:],
        ]
    )
    return packed, over_slots(pick_slots(dacts))


def begin_kernel(n_pieces, *refs):
    pieces, weights = refs[:n_pieces], refs[n_pieces : n_pieces + 3]
    pt_out, c_out, parts_out, *held, sems = refs[n_pieces + 3 :]
    copies = [
        pltpu.make_async_copy(w, h, sems.at[k])
        for k, (w, h) in enumerate(zip(weights, held))
    ]
    for copy in copies:
        copy.start()
    place(pieces, 0, pt_out, c_out)
    for copy in copies:
        copy.wait()
    parts_out[0], parts_out[1] = projections(pt_out[...], c_out[...], *held)


def begin(pieces, weights):
    blocks = sum(p.shape[0] for p in pieces)
    lanes, hidden = pieces[0].shape[2], weights[0].shape[1]
    vmem = pl.BlockSpec(memory_space=pltpu.VMEM)
    return pl.pallas_call(
        functools.partial(begin_kernel, len(pieces)),
        out_shape=(
            jax.ShapeDtypeStruct((blocks * 16, lanes), jnp.bfloat16),
            jax.ShapeDtypeStruct((blocks * 8, lanes), jnp.bfloat16),
            jax.ShapeDtypeStruct((2, blocks, 8, hidden), jnp.float32),
        )
        + tuple(jax.ShapeDtypeStruct(w.shape, w.dtype) for w in weights),
        in_specs=[vmem] * len(pieces) + [pl.BlockSpec(memory_space=pltpu.HBM)] * 3,
        out_specs=(vmem,) * 6,
        scratch_shapes=[pltpu.SemaphoreType.DMA((3,))],
        compiler_params=pltpu.CompilerParams(vmem_limit_bytes=50 * 2**20),
        cost_estimate=pl.CostEstimate(
            flops=blocks * 8 * 10 * SLOTS * lanes * hidden,
            bytes_accessed=sum(4 * w.size for w in weights),
            transcendentals=0,
        ),
    )(*pieces, *weights)


def finish_kernel(n_pieces, *refs):
    pieces, weights = refs[:n_pieces], refs[n_pieces : n_pieces + 3]
    pt_in, c_in, parts_in, pt_out, c_out, parts_out = refs[n_pieces + 3 :]
    blocks = parts_in.shape[1]
    pt_out[: blocks * 16] = pt_in[...]
    c_out[: blocks * 8] = c_in[...]
    parts_out[:, :blocks] = parts_in[...]
    place(pieces, blocks, pt_out, c_out)
    parts_out[0, blocks:], parts_out[1, blocks:] = projections(
        pt_out[blocks * 16 :], c_out[blocks * 8 :], *weights
    )


def finish(pieces, weights, pt, cot, parts):
    blocks = parts.shape[1] + sum(p.shape[0] for p in pieces)
    lanes, hidden = pieces[0].shape[2], weights[0].shape[1]
    vmem = pl.BlockSpec(memory_space=pltpu.VMEM)
    return pl.pallas_call(
        functools.partial(finish_kernel, len(pieces)),
        out_shape=(
            jax.ShapeDtypeStruct((blocks * 16, lanes), jnp.bfloat16),
            jax.ShapeDtypeStruct((blocks * 8, lanes), jnp.bfloat16),
            jax.ShapeDtypeStruct((2, blocks, 8, hidden), jnp.float32),
        ),
        in_specs=[vmem] * (len(pieces) + 6),
        out_specs=(vmem,) * 3,
        compiler_params=pltpu.CompilerParams(vmem_limit_bytes=VMEM_LIMIT),
    )(*pieces, *weights, pt, cot, parts)


def factors(gate, up, tgate, tup, dact):
    sig = 1.0 / (1.0 + jnp.exp(-gate))
    act = gate * sig
    first = sig * (1.0 + gate * (1.0 - sig))
    second = sig * (1.0 - sig) * (2.0 + gate * (1.0 - 2.0 * sig))
    dgate = dact * up * first
    dup = dact * act
    tdgate = dact * (tup * first + up * second * tgate)
    tdup = dact * first * tgate
    tact = tgate * first * up + act * tup
    return (dgate, dup, tdgate, tdup, tact)


def by_slot(x):
    rows = x.size // x.shape[-1]
    return jnp.concatenate(
        [only_slot(x, s).reshape(rows, x.shape[-1]) for s in range(SLOTS)], axis=1
    ).astype(jnp.bfloat16)


def middle_kernel(n_parts, groups, order, places, *refs):
    parts, (gate_w, up_w) = refs[:n_parts], refs[n_parts : n_parts + 2]
    factor_out, tact_out = refs[n_parts + 2 : n_parts + 4]
    own_out, others_out = refs[n_parts + 4], refs[n_parts + 5 :]
    packed, dact = (
        sum(
            (
                jnp.stack([p[k, at] for at in places]) if shift % 2 else p[k]
                for shift, p in enumerate(parts)
            ),
            0.0,
        )
        for k in range(2)
    )
    gate, up, tgate, tup = (over_slots(only_slot(packed, s)) for s in range(SLOTS))
    dgate, dup, tdgate, tdup, tact = factors(gate, up, tgate, tup, dact)
    blocks, _, hidden = gate.shape
    second = jnp.concatenate([tdgate, tdup], axis=2)
    pair = jnp.stack([second, jnp.concatenate([dgate, dup], axis=2)], axis=1)
    factor_out[...] = by_slot(pair)
    tact_out[...] = by_slot(tact)
    right = jnp.concatenate(
        [rows_for_slot(w[...], s) for s in range(SLOTS) for w in (gate_w, up_w)], axis=1
    )
    hvp = lax.dot_general(
        by_slot(second),
        right,
        (((1,), (1,)), ((), ())),
        preferred_element_type=jnp.float32,
    )
    hvp = hvp.reshape(blocks, 8, hvp.shape[1])
    inner = blocks // groups
    for k, at in enumerate(order):
        group, place_in = divmod(k, inner)
        out = others_out[group - 1] if group else own_out
        out[place_in] = hvp[at].astype(out.dtype)


def middle(parts, gate_w, up_w, groups, order, places):
    _, blocks, _, hidden = parts[0].shape
    lanes = gate_w.shape[0] // SLOTS
    vmem = pl.BlockSpec(memory_space=pltpu.VMEM)
    group = (blocks // groups, 8, lanes)
    return pl.pallas_call(
        functools.partial(middle_kernel, len(parts), groups, order, places),
        out_shape=(
            jax.ShapeDtypeStruct((blocks * 16, SLOTS * 2 * hidden), jnp.bfloat16),
            jax.ShapeDtypeStruct((blocks * 8, SLOTS * hidden), jnp.bfloat16),
            jax.ShapeDtypeStruct(group, jnp.float32),
        )
        + (jax.ShapeDtypeStruct(group, jnp.bfloat16),) * (groups - 1),
        in_specs=[vmem] * (len(parts) + 2),
        out_specs=(vmem,) * (groups + 2),
        compiler_params=pltpu.CompilerParams(vmem_limit_bytes=VMEM_LIMIT),
    )(*parts, gate_w, up_w)


def contract_first(left, right):
    return lax.dot_general(
        left, right, (((0,), (0,)), ((), ())), preferred_element_type=jnp.float32
    )


def up_grads_kernel(pt, factor, gate_out, up_out, gate_tiles, up_tiles, sems):
    tiles, _, hidden = gate_tiles.shape
    copies = []
    for m in range(tiles):
        both = contract_first(pt[:, m * LANES : (m + 1) * LANES], factor[...])
        for s in range(SLOTS):
            at, half = slice(s * LANES, (s + 1) * LANES), 2 * s * hidden
            gate_tiles[m, at] = both[:, half : half + hidden]
            up_tiles[m, at] = both[:, half + hidden : half + 2 * hidden]
        rows = slice(m * SLOTS * LANES, (m + 1) * SLOTS * LANES)
        for k, (tile, out) in enumerate(((gate_tiles, gate_out), (up_tiles, up_out))):
            copies.append(pltpu.make_async_copy(tile.at[m], out.at[rows], sems.at[m, k]))
            copies[-1].start()
    for copy in copies:
        copy.wait()


def up_grads(pt, factor):
    rows, lanes = pt.shape
    tiles, hidden = lanes // LANES, factor.shape[1] // (2 * SLOTS)
    out = jax.ShapeDtypeStruct((SLOTS * lanes, hidden), jnp.float32)
    vmem = pl.BlockSpec(memory_space=pltpu.VMEM)
    return pl.pallas_call(
        up_grads_kernel,
        out_shape=(out, out),
        in_specs=[vmem] * 2,
        out_specs=(pl.BlockSpec(memory_space=pltpu.HBM),) * 2,
        scratch_shapes=[
            pltpu.VMEM((tiles, SLOTS * LANES, hidden), jnp.float32),
            pltpu.VMEM((tiles, SLOTS * LANES, hidden), jnp.float32),
            pltpu.SemaphoreType.DMA((tiles, 2)),
        ],
        compiler_params=pltpu.CompilerParams(vmem_limit_bytes=VMEM_LIMIT),
        cost_estimate=pl.CostEstimate(
            flops=2 * pt.size * factor.shape[1],
            bytes_accessed=8 * SLOTS * lanes * hidden,
            transcendentals=0,
        ),
    )(pt, factor)


def down_grad_kernel(cot, tact, down_out, down_tiles, sems):
    tiles, hidden, _ = down_tiles.shape
    copies = []
    for m in range(tiles):
        down = contract_first(tact[...], cot[:, m * LANES : (m + 1) * LANES])
        for s in range(SLOTS):
            at = slice(s * LANES, (s + 1) * LANES)
            down_tiles[m, :, at] = down[s * hidden : (s + 1) * hidden]
        columns = slice(m * SLOTS * LANES, (m + 1) * SLOTS * LANES)
        copies.append(
            pltpu.make_async_copy(down_tiles.at[m], down_out.at[:, columns], sems.at[m])
        )
        copies[-1].start()
    for copy in copies:
        copy.wait()


def down_grad(cot, tact):
    lanes = cot.shape[1]
    tiles, hidden = lanes // LANES, tact.shape[1] // SLOTS
    vmem = pl.BlockSpec(memory_space=pltpu.VMEM)
    return pl.pallas_call(
        down_grad_kernel,
        out_shape=jax.ShapeDtypeStruct((hidden, SLOTS * lanes), jnp.float32),
        in_specs=[vmem] * 2,
        out_specs=pl.BlockSpec(memory_space=pltpu.HBM),
        scratch_shapes=[
            pltpu.VMEM((tiles, hidden, SLOTS * LANES), jnp.float32),
            pltpu.SemaphoreType.DMA((tiles,)),
        ],
        compiler_params=pltpu.CompilerParams(vmem_limit_bytes=VMEM_LIMIT),
        cost_estimate=pl.CostEstimate(
            flops=2 * cot.size * tact.shape[1],
            bytes_accessed=4 * SLOTS * lanes * hidden,
            transcendentals=0,
        ),
    )(cot, tact)


def solution(mesh):
    wide, narrow = mesh.shape["wide"], mesh.shape["narrow"]

    def local(primal_in, tangent_in, cotangent, gate_weight, up_weight, down_weight):
        weights = (gate_weight, up_weight, down_weight)
        early, late, order = gather_blocks(
            fold(primal_in, tangent_in, cotangent), (wide, narrow)
        )
        *first, gate_weight, up_weight, down_weight = begin(early, weights)
        weights = (gate_weight, up_weight, down_weight)
        pt, cot, part = finish(late, weights, *first)
        parts = [part]
        for shift in range(1, narrow):
            pairs = [(i, (i + shift) % narrow) for i in range(narrow)]
            parts.append(lax.ppermute(part, "narrow", pairs))
        finest = levels_of(wide)[-1]
        groups, places = finest[1], aligned(order, finest)
        factor, tact, *hvp = middle(
            parts, gate_weight, up_weight, groups, order, places
        )
        gate_grad, up_grad = up_grads(pt, factor)
        total = scatter_sum(hvp, (wide, narrow), gate_grad)
        input_hvp = unfold(total[0].astype(jnp.bfloat16))
        return (input_hvp, gate_grad, up_grad, down_grad(cot, tact))

    return jax.shard_map(
        local,
        mesh=mesh,
        in_specs=(
            P("wide", "narrow"),
            P("wide", "narrow"),
            P("wide", "narrow"),
            P("narrow", "wide"),
            P("narrow", "wide"),
            P("wide", "narrow"),
        ),
        out_specs=(
            P("wide", "narrow"),
            P("narrow", "wide"),
            P("narrow", "wide"),
            P("wide", "narrow"),
        ),
        check_vma=False,
    )
```

```python
import functools

import jax
import jax.numpy as jnp
from jax import lax
from jax.experimental import pallas as pl
from jax.experimental.pallas import tpu as pltpu
from jax.sharding import PartitionSpec as P

SLOTS = 4
LANES = 128
VMEM_LIMIT = 24 * 2**20


def levels_of(size):
    levels, stride = [], 1
    while stride < size:
        rest = size // stride
        radix = next(r for r in (4, 2, 3, 5, 7, rest) if rest % r == 0)
        levels.append((stride, radix))
        stride *= radix
    return levels[::-1]


def partner(index, stride, radix, offset):
    digit = index // stride % radix
    if radix & (radix - 1) == 0:
        other = digit ^ offset
    else:
        other = (digit + offset) % radix
    return index + (other - digit) * stride


def turned(offset, level, core):
    stride, radix = level
    if stride == 1 and radix == 4 and core % 2 and offset in (1, 2):
        return 3 - offset
    return offset


def pairs_of(sizes, level, offset):
    wide, narrow = sizes
    return [
        (i * narrow + c, partner(i, *level, turned(offset, level, c)) * narrow + c)
        for i in range(wide)
        for c in range(narrow)
    ]


def fetch(value, sizes, level, offset):
    pairs = [(there, here) for here, there in pairs_of(sizes, level, offset)]
    return lax.ppermute(value, ("wide", "narrow"), pairs)


def deliver(value, sizes, level, offset):
    return lax.ppermute(value, ("wide", "narrow"), pairs_of(sizes, level, offset))


def after(value, earlier):
    return lax.optimization_barrier((value, earlier))[0]


def offsets_of(radix):
    return range(radix - 1, 0, -1)


def aligned(order, level):
    inner = len(order) // level[1]
    slots = {o: k + 1 for k, o in enumerate(offsets_of(level[1]))} | {0: 0}
    places = [0] * len(order)
    for offset, slot in slots.items():
        other = slots[turned(offset, level, 1)]
        for k in range(inner):
            places[order[slot * inner + k]] = order[other * inner + k]
    return places


def gather_blocks(own, sizes):
    early, late, count = [(own, [0])], [], 1
    before = None
    for level in levels_of(sizes[0]):
        rest = early[1:] + late
        offsets = list(offsets_of(level[1]))
        slots = {o: count * (k + 1) for k, o in enumerate(offsets)}
        starts = offsets[::-1] if rest else offsets
        mine = {o: fetch(own, sizes, level, o) for o in starts}
        late = [(mine[o], [slots[o]]) for o in starts]
        early = [(own, [0])]
        if rest:
            held = join(rest)
            step, near = before
            far = join([piece for piece in rest if piece[1] != [near]])
            early, late = early + [held] + late, []
            came = []
            for o, first in zip(offsets, starts[:1] * 2 + starts[1:]):
                part, ids = far if o & (o - 1) else held
                block = fetch(after(part, mine[first]), sizes, level, o)
                came.append((block, [slots[o] + i for i in ids]))
            for o in offsets:
                if o & (o - 1):
                    block = fetch(mine[o], sizes, step, 1)
                    came.append((block, [slots[o] + near]))
            late += [came[k] for k in (1, 2, 0, 3) if k < len(came)]
        before = level, slots[1]
        count *= level[1]
    pieces = early + late
    ids = sum((ids for _, ids in pieces), [])
    order = [ids.index(k) for k in range(count)]
    return [block for block, _ in early], [block for block, _ in late], order


def join(pieces):
    blocks = jnp.concatenate([block for block, _ in pieces])
    return blocks, sum((ids for _, ids in pieces), [])


def scatter_sum(groups, sizes, beside):
    for level in levels_of(sizes[0])[::-1]:
        if len(groups) == 1:
            groups = jnp.split(after(groups[0], beside), level[1])
        came = [
            deliver(group.astype(jnp.bfloat16), sizes, level, o)
            for o, group in zip(offsets_of(level[1]), groups[1:])
        ]
        total = groups[0]
        for block in came[::-1]:
            total = total + block.astype(jnp.float32)
        groups = [total]
    return groups[0]


def fold(*rows):
    stacked = lax.optimization_barrier(jnp.stack(rows))
    count, tokens, width = stacked.shape
    split = stacked.reshape(count, tokens, width // (SLOTS * LANES), SLOTS, LANES)
    return split.transpose(0, 3, 1, 2, 4).reshape(1, -1, width // SLOTS)


def unfold(rows):
    tokens = rows.shape[0] // SLOTS
    split = rows.reshape(SLOTS, tokens, rows.shape[1] // LANES, LANES)
    return split.transpose(1, 2, 0, 3).reshape(tokens, rows.shape[1] * SLOTS)


def slot_of(shape, axis):
    return lax.broadcasted_iota(jnp.int32, shape, axis) // 2


def rows_for_slot(weight, slot):
    height, width = weight.shape
    split = weight.reshape(height // (SLOTS * LANES), SLOTS, LANES, width)
    return split[:, slot].reshape(height // SLOTS, width)


def over_slots(x):
    axis = x.ndim - 2
    x = x + pltpu.roll(x, 4, axis)
    return x + pltpu.roll(x, 2, axis)


def pick_slots(parts):
    slot = slot_of(parts[0].shape, parts[0].ndim - 2)
    result = parts[0]
    for s in range(1, SLOTS):
        result = jnp.where(slot == s, parts[s], result)
    return result


def only_slot(x, s):
    return jnp.where(slot_of(x.shape, x.ndim - 2) == s, x, 0.0)


def place(pieces, at, pt_out, c_out):
    for piece in pieces:
        for i in range(piece.shape[0]):
            pt_out[at * 16 : at * 16 + 16] = piece[i, 0:16]
            c_out[at * 8 : at * 8 + 8] = piece[i, 16:24]
            at += 1


def projections(pt, cot, gate_w, up_w, down_w):
    blocks, hidden = cot.shape[0] // 8, gate_w.shape[1]
    acts, dacts = [], []
    for s in range(SLOTS):
        weights = jnp.concatenate(
            [rows_for_slot(gate_w[...], s), rows_for_slot(up_w[...], s)], axis=1
        )
        acts.append(
            jnp.dot(pt, weights, preferred_element_type=jnp.float32).reshape(
                2 * blocks, 8, 2 * hidden
            )
        )
        columns = [
            down_w[:, j * LANES : (j + 1) * LANES]
            for j in range(s, down_w.shape[1] // LANES, SLOTS)
        ]
        dacts.append(
            lax.dot_general(
                cot,
                jnp.concatenate(columns, axis=1),
                (((1,), (1,)), ((), ())),
                preferred_element_type=jnp.float32,
            ).reshape(blocks, 8, hidden)
        )
    act = over_slots(pick_slots(acts)).reshape(blocks, 2, 8, 2 * hidden)
    packed = pick_slots(
        [
            act[:, 0, :, :hidden],
            act[:, 0, :, hidden:],
            act[:, 1, :, :hidden],
            act[:, 1, :, hidden:],
        ]
    )
    return packed, over_slots(pick_slots(dacts))


def begin_kernel(n_pieces, *refs):
    pieces, weights = refs[:n_pieces], refs[n_pieces : n_pieces + 3]
    pt_out, c_out, parts_out, *held, sems = refs[n_pieces + 3 :]
    copies = [
        pltpu.make_async_copy(w, h, sems.at[k])
        for k, (w, h) in enumerate(zip(weights, held))
    ]
    for copy in copies:
        copy.start()
    place(pieces, 0, pt_out, c_out)
    for copy in copies:
        copy.wait()
    parts_out[0], parts_out[1] = projections(pt_out[...], c_out[...], *held)


def begin(pieces, weights):
    blocks = sum(p.shape[0] for p in pieces)
    lanes, hidden = pieces[0].shape[2], weights[0].shape[1]
    vmem = pl.BlockSpec(memory_space=pltpu.VMEM)
    return pl.pallas_call(
        functools.partial(begin_kernel, len(pieces)),
        out_shape=(
            jax.ShapeDtypeStruct((blocks * 16, lanes), jnp.bfloat16),
            jax.ShapeDtypeStruct((blocks * 8, lanes), jnp.bfloat16),
            jax.ShapeDtypeStruct((2, blocks, 8, hidden), jnp.float32),
        )
        + tuple(jax.ShapeDtypeStruct(w.shape, w.dtype) for w in weights),
        in_specs=[vmem] * len(pieces) + [pl.BlockSpec(memory_space=pltpu.HBM)] * 3,
        out_specs=(vmem,) * 6,
        scratch_shapes=[pltpu.SemaphoreType.DMA((3,))],
        compiler_params=pltpu.CompilerParams(vmem_limit_bytes=50 * 2**20),
        cost_estimate=pl.CostEstimate(
            flops=blocks * 8 * 10 * SLOTS * lanes * hidden,
            bytes_accessed=sum(4 * w.size for w in weights),
            transcendentals=0,
        ),
    )(*pieces, *weights)


def finish_kernel(n_pieces, *refs):
    pieces, weights = refs[:n_pieces], refs[n_pieces : n_pieces + 3]
    pt_in, c_in, parts_in, pt_out, c_out, parts_out = refs[n_pieces + 3 :]
    blocks = parts_in.shape[1]
    pt_out[: blocks * 16] = pt_in[...]
    c_out[: blocks * 8] = c_in[...]
    parts_out[:, :blocks] = parts_in[...]
    place(pieces, blocks, pt_out, c_out)
    parts_out[0, blocks:], parts_out[1, blocks:] = projections(
        pt_out[blocks * 16 :], c_out[blocks * 8 :], *weights
    )


def finish(pieces, weights, pt, cot, parts):
    blocks = parts.shape[1] + sum(p.shape[0] for p in pieces)
    lanes, hidden = pieces[0].shape[2], weights[0].shape[1]
    vmem = pl.BlockSpec(memory_space=pltpu.VMEM)
    return pl.pallas_call(
        functools.partial(finish_kernel, len(pieces)),
        out_shape=(
            jax.ShapeDtypeStruct((blocks * 16, lanes), jnp.bfloat16),
            jax.ShapeDtypeStruct((blocks * 8, lanes), jnp.bfloat16),
            jax.ShapeDtypeStruct((2, blocks, 8, hidden), jnp.float32),
        ),
        in_specs=[vmem] * (len(pieces) + 6),
        out_specs=(vmem,) * 3,
        compiler_params=pltpu.CompilerParams(vmem_limit_bytes=VMEM_LIMIT),
    )(*pieces, *weights, pt, cot, parts)


def factors(gate, up, tgate, tup, dact):
    sig = 1.0 / (1.0 + jnp.exp(-gate))
    act = gate * sig
    first = sig * (1.0 + gate * (1.0 - sig))
    second = sig * (1.0 - sig) * (2.0 + gate * (1.0 - 2.0 * sig))
    dgate = dact * up * first
    dup = dact * act
    tdgate = dact * (tup * first + up * second * tgate)
    tdup = dact * first * tgate
    tact = tgate * first * up + act * tup
    return (dgate, dup, tdgate, tdup, tact)


def by_slot(x):
    rows = x.size // x.shape[-1]
    return jnp.concatenate(
        [only_slot(x, s).reshape(rows, x.shape[-1]) for s in range(SLOTS)], axis=1
    ).astype(jnp.bfloat16)


def middle_kernel(n_parts, groups, order, places, *refs):
    parts, (gate_w, up_w) = refs[:n_parts], refs[n_parts : n_parts + 2]
    factor_out, tact_out = refs[n_parts + 2 : n_parts + 4]
    own_out, others_out = refs[n_parts + 4], refs[n_parts + 5 :]
    packed, dact = (
        sum(
            (
                jnp.stack([p[k, at] for at in places]) if shift % 2 else p[k]
                for shift, p in enumerate(parts)
            ),
            0.0,
        )
        for k in range(2)
    )
    gate, up, tgate, tup = (over_slots(only_slot(packed, s)) for s in range(SLOTS))
    dgate, dup, tdgate, tdup, tact = factors(gate, up, tgate, tup, dact)
    blocks, _, hidden = gate.shape
    second = jnp.concatenate([tdgate, tdup], axis=2)
    pair = jnp.stack([second, jnp.concatenate([dgate, dup], axis=2)], axis=1)
    factor_out[...] = by_slot(pair)
    tact_out[...] = by_slot(tact)
    right = jnp.concatenate(
        [rows_for_slot(w[...], s) for s in range(SLOTS) for w in (gate_w, up_w)], axis=1
    )
    hvp = lax.dot_general(
        by_slot(second),
        right,
        (((1,), (1,)), ((), ())),
        preferred_element_type=jnp.float32,
    )
    hvp = hvp.reshape(blocks, 8, hvp.shape[1])
    inner = blocks // groups
    for k, at in enumerate(order):
        group, place_in = divmod(k, inner)
        out = others_out[group - 1] if group else own_out
        out[place_in] = hvp[at].astype(out.dtype)


def middle(parts, gate_w, up_w, groups, order, places):
    _, blocks, _, hidden = parts[0].shape
    lanes = gate_w.shape[0] // SLOTS
    vmem = pl.BlockSpec(memory_space=pltpu.VMEM)
    group = (blocks // groups, 8, lanes)
    return pl.pallas_call(
        functools.partial(middle_kernel, len(parts), groups, order, places),
        out_shape=(
            jax.ShapeDtypeStruct((blocks * 16, SLOTS * 2 * hidden), jnp.bfloat16),
            jax.ShapeDtypeStruct((blocks * 8, SLOTS * hidden), jnp.bfloat16),
            jax.ShapeDtypeStruct(group, jnp.float32),
        )
        + (jax.ShapeDtypeStruct(group, jnp.bfloat16),) * (groups - 1),
        in_specs=[vmem] * (len(parts) + 2),
        out_specs=(vmem,) * (groups + 2),
        compiler_params=pltpu.CompilerParams(vmem_limit_bytes=VMEM_LIMIT),
    )(*parts, gate_w, up_w)


def contract_first(left, right):
    return lax.dot_general(
        left, right, (((0,), (0,)), ((), ())), preferred_element_type=jnp.float32
    )


def up_grads_kernel(pt, factor, gate_out, up_out, gate_tiles, up_tiles, sems):
    tiles, _, hidden = gate_tiles.shape
    copies = []
    for m in range(tiles):
        both = contract_first(pt[:, m * LANES : (m + 1) * LANES], factor[...])
        for s in range(SLOTS):
            at, half = slice(s * LANES, (s + 1) * LANES), 2 * s * hidden
            gate_tiles[m, at] = both[:, half : half + hidden]
            up_tiles[m, at] = both[:, half + hidden : half + 2 * hidden]
        rows = slice(m * SLOTS * LANES, (m + 1) * SLOTS * LANES)
        for k, (tile, out) in enumerate(((gate_tiles, gate_out), (up_tiles, up_out))):
            copies.append(pltpu.make_async_copy(tile.at[m], out.at[rows], sems.at[m, k]))
            copies[-1].start()
    for copy in copies:
        copy.wait()


def up_grads(pt, factor):
    rows, lanes = pt.shape
    tiles, hidden = lanes // LANES, factor.shape[1] // (2 * SLOTS)
    out = jax.ShapeDtypeStruct((SLOTS * lanes, hidden), jnp.float32)
    vmem = pl.BlockSpec(memory_space=pltpu.VMEM)
    return pl.pallas_call(
        up_grads_kernel,
        out_shape=(out, out),
        in_specs=[vmem] * 2,
        out_specs=(pl.BlockSpec(memory_space=pltpu.HBM),) * 2,
        scratch_shapes=[
            pltpu.VMEM((tiles, SLOTS * LANES, hidden), jnp.float32),
            pltpu.VMEM((tiles, SLOTS * LANES, hidden), jnp.float32),
            pltpu.SemaphoreType.DMA((tiles, 2)),
        ],
        compiler_params=pltpu.CompilerParams(vmem_limit_bytes=VMEM_LIMIT),
        cost_estimate=pl.CostEstimate(
            flops=2 * pt.size * factor.shape[1],
            bytes_accessed=8 * SLOTS * lanes * hidden,
            transcendentals=0,
        ),
    )(pt, factor)


def down_grad_kernel(cot, tact, down_out, down_tiles, sems):
    tiles, hidden, _ = down_tiles.shape
    copies = []
    for m in range(tiles):
        down = contract_first(tact[...], cot[:, m * LANES : (m + 1) * LANES])
        for s in range(SLOTS):
            at = slice(s * LANES, (s + 1) * LANES)
            down_tiles[m, :, at] = down[s * hidden : (s + 1) * hidden]
        columns = slice(m * SLOTS * LANES, (m + 1) * SLOTS * LANES)
        copies.append(
            pltpu.make_async_copy(down_tiles.at[m], down_out.at[:, columns], sems.at[m])
        )
        copies[-1].start()
    for copy in copies:
        copy.wait()


def down_grad(cot, tact):
    lanes = cot.shape[1]
    tiles, hidden = lanes // LANES, tact.shape[1] // SLOTS
    vmem = pl.BlockSpec(memory_space=pltpu.VMEM)
    return pl.pallas_call(
        down_grad_kernel,
        out_shape=jax.ShapeDtypeStruct((hidden, SLOTS * lanes), jnp.float32),
        in_specs=[vmem] * 2,
        out_specs=pl.BlockSpec(memory_space=pltpu.HBM),
        scratch_shapes=[
            pltpu.VMEM((tiles, hidden, SLOTS * LANES), jnp.float32),
            pltpu.SemaphoreType.DMA((tiles,)),
        ],
        compiler_params=pltpu.CompilerParams(vmem_limit_bytes=VMEM_LIMIT),
        cost_estimate=pl.CostEstimate(
            flops=2 * cot.size * tact.shape[1],
            bytes_accessed=4 * SLOTS * lanes * hidden,
            transcendentals=0,
        ),
    )(cot, tact)


def solution(mesh):
    wide, narrow = mesh.shape["wide"], mesh.shape["narrow"]

    def local(primal_in, tangent_in, cotangent, gate_weight, up_weight, down_weight):
        weights = (gate_weight, up_weight, down_weight)
        early, late, order = gather_blocks(
            fold(primal_in, tangent_in, cotangent), (wide, narrow)
        )
        *first, gate_weight, up_weight, down_weight = begin(early, weights)
        weights = (gate_weight, up_weight, down_weight)
        pt, cot, part = finish(late, weights, *first)
        parts = [part]
        for shift in range(1, narrow):
            pairs = [(i, (i + shift) % narrow) for i in range(narrow)]
            parts.append(lax.ppermute(part, "narrow", pairs))
        finest = levels_of(wide)[-1]
        groups, places = finest[1], aligned(order, finest)
        factor, tact, *hvp = middle(
            parts, gate_weight, up_weight, groups, order, places
        )
        gate_grad, up_grad = up_grads(pt, factor)
        total = scatter_sum(hvp, (wide, narrow), gate_grad)
        input_hvp = unfold(total[0].astype(jnp.bfloat16))
        return (input_hvp, gate_grad, up_grad, down_grad(cot, tact))

    return jax.shard_map(
        local,
        mesh=mesh,
        in_specs=(
            P("wide", "narrow"),
            P("wide", "narrow"),
            P("wide", "narrow"),
            P("narrow", "wide"),
            P("narrow", "wide"),
            P("wide", "narrow"),
        ),
        out_specs=(
            P("wide", "narrow"),
            P("narrow", "wide"),
            P("narrow", "wide"),
            P("wide", "narrow"),
        ),
        check_vma=False,
    )
```
